256 devices in a mesh: gz: 8 (over x, core), xy: 32 (over y, z).
Axes of the slice: x: 4, y: 4, z: 8, core: 2. Of those that a mesh axis runs over, the one named last changes fastest.
Arguments:
- residual: float32 [512, 32, 1024], P('xy', None, 'gz'), may hold values from -6 to 6
- eigen_vectors: float32 [3, 10, 10], replicated, may hold values from -2 to 2
- eigen_values: float32 [3, 10], replicated, may hold values from 0.2 to 5
- element_scale: float32 [64, 4, 128], P('xy', None, 'gz'), may hold values from 0.5 to 4
- vertex_map: int32 [64, 4, 128], P('xy', None, 'gz'), may hold values from 0 to 511
- leaf_columns: float32 [131072, 512], P(('gz', 'xy')), may hold values from -0.25 to 0.25
- separator_columns: float32 [131072, 3072], P(('gz', 'xy')), may hold values from -0.25 to 0.25
- separator_mask: int32 [256, 6], P(('gz', 'xy')), may hold values 0 or 1
Outputs:
- preconditioned: float32 [512, 32, 1024], P('xy', None, 'gz')
- coarse_solution: float32 [131072], P(('gz', 'xy'))
The draws below stay inside these ranges and needn't reach their ends.
Inputs may be any that keep to these rules, and one draw needn't show every extreme that they name: vertex_map names a vertex of the element's own device.
All inputs are finite; a program needn't handle non-finite values. No bound on the sum of `separator_mask` on one device may be relied on, other than what follows from the above.
Results may differ from the reference program's by a relative error of at most 0.0001.
Values sent between devices are 32-bit elements; how exact they have to be, the bound alone decides.
No kernel may reach another device: no remote copies, remote signals or barrier semaphores. Data moves between devices by JAX's collectives and lax.ppermute only.
A program may use at most 128 MiB of HBM per device.

```python
import math
import jax
import jax.numpy as jnp
from jax import lax

NP = 8
EX = 2
EY = 4
EZ = 16
VERTS = 512
SW = 512
LEVELS = 6
EXG = 64
EZG = 128
NXP = 512
NYP = 32
NZP = 1024
NC = 131072
N_XY = 32
DEVICES = 256


def touch_ends(drawn, rng, smallest, top_value):
    longest = drawn.shape.index(max(drawn.shape))
    spots = []
    for shift in (0, 1):
        where = [jax.random.randint(jax.random.fold_in(rng, axis), (), 0, length) for axis, length in enumerate(drawn.shape)]
        where[longest] = (where[longest] + shift) % drawn.shape[longest]
        spots.append(tuple(where))
    return drawn.at[spots[0]].set(smallest).at[spots[1]].set(top_value)


def levels(key, shape, cuts, low, top_value):
    level = 1.0
    for axis_at, parts in cuts:
        heights = jax.random.uniform(jax.random.fold_in(jax.random.fold_in(key, 6), axis_at), (parts,), jnp.float32, low / len(cuts), top_value / len(cuts))
        level = level * jnp.repeat(jnp.exp(heights), shape[axis_at] // parts).reshape((-1,) + (1,) * (len(shape) - 1 - axis_at))
    return level


def centred(key, shape, width, limit, cuts=(), kind=jnp.bfloat16):
    values = jax.random.normal(key, shape, jnp.float32) * width
    if len(cuts) > 0:
        values = levels(key, shape, cuts, -0.22, 0.18) * values
    return jnp.clip(values, min=-limit, max=limit).astype(kind)


def setup_inputs(seed: int = 0) -> dict:
    streams_of = jax.random.split(jax.random.key(seed), 9)
    residual = centred(streams_of[0], (NXP, NYP, NZP), 1.0, 6.0, ((0, 32), (2, 8)), jnp.float32)
    eigen_vectors = centred(streams_of[1], (3, NP + 2, NP + 2), (NP + 2) ** -0.5, 2.0, (), jnp.float32)
    eigen_values = jnp.clip(jnp.exp(jax.random.uniform(streams_of[2], (3, NP + 2), jnp.float32, math.log(0.2), math.log(5.0))), 0.2, 5.0)
    element_scale = jnp.clip(jnp.exp(math.log(4.0) - 2.0794415 * jax.random.uniform(streams_of[3], (EXG, EY, EZG), jnp.float32) ** levels(streams_of[3], (EXG, EY, EZG), ((0, 32), (2, 8)), -0.2, 0.2)), 0.5, 4.0)
    vertex_map = touch_ends(jax.random.randint(streams_of[4], (EXG, EY, EZG), 0, VERTS), jax.random.fold_in(streams_of[4], 1), 0, VERTS - 1).astype(jnp.int32)
    leaf_columns = centred(streams_of[5], (NC, VERTS), VERTS ** -0.5, 0.25, ((0, 256),), jnp.float32)
    separator_columns = centred(streams_of[6], (NC, LEVELS * SW), VERTS ** -0.5, 0.25, ((0, 256),), jnp.float32)
    separator_mask = touch_ends((jax.random.randint(streams_of[7], (DEVICES, LEVELS), 0, 4) < 3).astype(jnp.int32), jax.random.fold_in(streams_of[7], 1), 0, 1)
    return dict(residual=residual, eigen_vectors=eigen_vectors, eigen_values=eigen_values, element_scale=element_scale, vertex_map=vertex_map, leaf_columns=leaf_columns, separator_columns=separator_columns, separator_mask=separator_mask)


HIGH = lax.Precision.HIGHEST


def extract(source, axis, count):
    pieces = [lax.slice_in_dim(source, offset, offset + NP * (count - 1) + 1, NP, axis) for offset in range(NP + 2)]
    return jnp.stack(pieces, axis=axis + 1)


def local_solve(padded, vectors, values, scale):
    count_x, count_y, count_z = scale.shape
    blocks = extract(padded, 0, count_x)
    section = jnp.einsum("om,aoyz->amyz", vectors[0], blocks, precision=HIGH)
    blocks = extract(section, 2, count_y)
    section = jnp.einsum("on,ambox->ambnx", vectors[1], blocks, precision=HIGH)
    blocks = extract(section, 4, count_z)
    section = jnp.einsum("op,ambnco->ambncp", vectors[2], blocks, precision=HIGH)
    denom = values[0][:, None, None] + values[1][None, :, None] + values[2][None, None, :]
    denom = scale[:, None, :, None, :, None] * denom[None, :, None, :, None, :]
    section = section / denom
    inner = vectors[:, 1:NP + 1, :]
    section = jnp.einsum("im,ambncp->aibncp", inner[0], section, precision=HIGH)
    section = jnp.einsum("jn,aibncp->aibjcp", inner[1], section, precision=HIGH)
    section = jnp.einsum("kp,aibjcp->aibjck", inner[2], section, precision=HIGH)
    return section.reshape(count_x * NP, count_y * NP, count_z * NP)


def reference(residual, eigen_vectors, eigen_values, element_scale, vertex_map, leaf_columns, separator_columns, separator_mask):
    padded = jnp.pad(residual, 1)

    def slab(index):
        piece = lax.dynamic_slice_in_dim(padded, index * NP, NP + 2, 0)
        scale = lax.dynamic_slice_in_dim(element_scale, index, 1, 0)
        return local_solve(piece, eigen_vectors, eigen_values, scale)

    local = lax.map(slab, jnp.arange(EXG, dtype=jnp.int32)).reshape(NXP, NYP, NZP)
    sums = residual.reshape(EXG, NP, EY, NP, EZG, NP).sum(axis=(1, 3, 5)) / float(NP ** 3)
    col_a = jnp.arange(EXG, dtype=jnp.int32)[:, None, None] // EX
    col_c = jnp.arange(EZG, dtype=jnp.int32)[None, None, :] // EZ
    device = col_c * N_XY + col_a
    global_id = (device * VERTS + vertex_map).astype(jnp.int32)
    coarse_rhs = jax.ops.segment_sum(sums.reshape(-1), global_id.reshape(-1), num_segments=NC)
    rhs_dev = coarse_rhs.reshape(DEVICES, VERTS)
    leaves = leaf_columns.reshape(DEVICES, VERTS, VERTS)
    leaf_alpha = jnp.einsum("dvw,dv->dw", leaves, rhs_dev, precision=HIGH)
    solution = jnp.einsum("dvw,dw->dv", leaves, leaf_alpha, precision=HIGH)
    seps = separator_columns.reshape(DEVICES, VERTS, LEVELS, SW) * separator_mask.astype(jnp.float32)[:, None, :, None]
    for level in range(LEVELS):
        group = DEVICES if level == LEVELS - 1 else 2 ** (level + 1)
        factor = float(group) ** -0.25
        column = seps[:, :, level, :] * factor
        partial_value = jnp.einsum("dvs,dv->ds", column, rhs_dev, precision=HIGH)
        totals = partial_value.reshape(DEVICES // group, group, SW).sum(axis=1)
        alpha = jnp.repeat(totals, group, axis=0)
        solution = solution + jnp.einsum("dvs,ds->dv", column, alpha, precision=HIGH)
    coarse_solution = solution.reshape(-1)
    per_element = coarse_solution[global_id]
    spread = jnp.broadcast_to(per_element[:, None, :, None, :, None], (EXG, NP, EY, NP, EZG, NP)).reshape(NXP, NYP, NZP)
    return local + spread, coarse_solution
```

```python
import functools

import jax
import jax.numpy as jnp
from jax import lax
from jax.experimental import pallas as pl
from jax.experimental.pallas import tpu as pltpu
from jax.sharding import PartitionSpec as P

NP = 8
LEVELS = 6
EX, EY, EZ = 2, 4, 16
VERTS = 512
SW = 512
ELEMS = EX * EY * EZ
NX, NY, NZ = EX * NP, EY * NP, EZ * NP
PTS = NP + 2
CHUNKS = 8
ROWS = VERTS // CHUNKS

F32 = jnp.float32
BF16 = jnp.bfloat16
HIGH = lax.Precision.HIGHEST
VMEM = pl.BlockSpec(memory_space=pltpu.VMEM)
SMEM = pl.BlockSpec(memory_space=pltpu.SMEM)
ANY = pl.BlockSpec(memory_space=pl.ANY)
PARAMS = pltpu.CompilerParams(vmem_limit_bytes=40 * 1024 * 1024)
NN = (((1,), (0,)), ((), ()))
NT = (((1,), (1,)), ((), ()))


def dot(a, b, dims=NN):
    return lax.dot_general(a, b, dims, precision=HIGH, preferred_element_type=F32)


def bdot(a, b, dims=NN):
    return lax.dot_general(a, b, dims, preferred_element_type=F32)


def split(a):
    hi = a.astype(BF16)
    return hi, (a - hi.astype(F32)).astype(BF16)


def dot3(a, b, dims=NN):
    return bdot(a[0], b[0], dims) + (bdot(a[0], b[1], dims) + bdot(a[1], b[0], dims))


def iota(shape, axis):
    return lax.broadcasted_iota(jnp.int32, shape, axis)


def div_mod(values, by):
    quotient = jnp.floor((values.astype(F32) + 0.5) * (1.0 / by)).astype(jnp.int32)
    return quotient, values - quotient * by


def mark(condition):
    return condition.astype(F32)


def face_kernel(r_ref, low_ref, high_ref):
    flat = r_ref[...].reshape(NX * NY, NZ)
    row, lane = iota((8, NZ), 0), iota((8, NZ), 1)
    pick = mark(((row == 0) & (lane == 0)) | ((row == 1) & (lane == NZ - 1)))
    faces = dot(pick, flat, NT)
    low_ref[...] = faces[0:1]
    high_ref[...] = faces[1:2]


def edge_kernel(r_ref, zlow_ref, zhigh_ref, low_ref, high_ref):
    for at, out in ((0, low_ref), (NX - 1, high_ref)):
        out[0:NY, :] = r_ref[at]
        out[NY : NY + 8, :] = jnp.zeros((8, NZ), F32)
        out[NY : NY + 1, 0:NY] = zlow_ref[0:1, at * NY : at * NY + NY]
        out[NY + 1 : NY + 2, 0:NY] = zhigh_ref[0:1, at * NY : at * NY + NY]


def onehot_of(vm_ref):
    vm = jnp.concatenate([vm_ref[0], vm_ref[1]], axis=0).astype(F32)
    spread = mark(iota((EZ, ELEMS), 0) == (iota((EZ, ELEMS), 1) & (EZ - 1)))
    wide = dot(vm, spread)
    mine = (iota((8, ELEMS), 1) >> 4) == iota((8, ELEMS), 0)
    row = jnp.sum(jnp.where(mine, wide, 0.0), axis=0, keepdims=True)
    return mark(iota((VERTS, ELEMS), 0).astype(F32) == row)


def factor(level):
    group = 256 if level == LEVELS - 1 else 2 ** (level + 1)
    return float(group) ** (-0.25)


def partial_kernel(r_ref, vm_ref, mask_ref, q_hbm, out_ref, b_ref, q_ref, sem):
    copies = []
    for c in range(CHUNKS):
        rows = pl.ds(c * ROWS, ROWS)
        copies.append(pltpu.make_async_copy(q_hbm.at[rows], q_ref.at[rows], sem.at[c]))
        copies[-1].start()
    sums = []
    for a in range(EX):
        total = r_ref[a * NP]
        for i in range(1, NP):
            total = total + r_ref[a * NP + i]
        sums.append(jnp.sum(total.reshape(EY, NP, NZ), axis=1))
    sums = jnp.concatenate(sums, axis=0)
    tall = jnp.broadcast_to(sums[:, None, :], (8, EZ, NZ)).reshape(ELEMS, NZ)
    own = (iota((ELEMS, NZ), 1) >> 3) == (iota((ELEMS, NZ), 0) & (EZ - 1))
    tall = jnp.where(own, tall, 0.0)
    means = dot(tall, jnp.full((NZ, NZ), 1.0 / NP**3, F32))
    b_ref[...] = dot(onehot_of(vm_ref), means)
    acc = [jnp.zeros((8, 128), F32) for _ in range(LEVELS * SW // 128)]
    for c in range(CHUNKS):
        copies[c].wait()
        for g in range(ROWS // 8):
            at = c * ROWS + g * 8
            b = b_ref[at : at + 8, :]
            for t in range(len(acc)):
                acc[t] = acc[t] + q_ref[at : at + 8, t * 128 : (t + 1) * 128] * b
    for level in range(LEVELS):
        scale = mask_ref[0, level].astype(F32) * factor(level)
        for k in range(SW // 128):
            total = jnp.sum(acc[level * (SW // 128) + k], axis=0, keepdims=True)
            out_ref[level : level + 1, k * 128 : (k + 1) * 128] = total * scale


def middle_kernel(mask_ref, alpha_ref, b_ref, leaf_ref, q_hbm, out_ref, q_ref, sem):
    width = (LEVELS - 1) * SW
    copies = []
    for c in range(CHUNKS):
        rows = pl.ds(c * ROWS, ROWS)
        copies.append(
            pltpu.make_async_copy(q_hbm.at[rows, pl.ds(0, width)], q_ref.at[rows], sem.at[c])
        )
        copies[-1].start()
    tiles = VERTS // 128
    acc = [jnp.zeros((8, 128), F32) for _ in range(tiles)]
    for g in range(VERTS // 8):
        b = b_ref[g * 8 : g * 8 + 8, :]
        for t in range(tiles):
            acc[t] = acc[t] + leaf_ref[g * 8 : g * 8 + 8, t * 128 : (t + 1) * 128] * b
    leaf_alpha = [jnp.sum(acc[t], axis=0, keepdims=True) for t in range(tiles)]
    alpha = []
    for level in range(LEVELS - 1):
        scale = mask_ref[0, level].astype(F32) * factor(level)
        for k in range(SW // 128):
            alpha.append(alpha_ref[level : level + 1, k * 128 : (k + 1) * 128] * scale)
    for c in range(CHUNKS):
        copies[c].wait()
        rows = slice(c * ROWS, (c + 1) * ROWS)
        total = leaf_ref[rows, 0:128] * leaf_alpha[0]
        for t in range(1, tiles):
            total = total + leaf_ref[rows, t * 128 : (t + 1) * 128] * leaf_alpha[t]
        for t in range(len(alpha)):
            total = total + q_ref[rows, t * 128 : (t + 1) * 128] * alpha[t]
        out_ref[rows, :] = total


def final_kernel(mask_ref, alpha_ref, base_ref, local_ref, vm_ref, q_hbm, out_ref, sol_ref, q_ref, sem):
    copy = pltpu.make_async_copy(q_hbm.at[:, pl.ds((LEVELS - 1) * SW, SW)], q_ref, sem.at[0])
    copy.start()
    onehot = onehot_of(vm_ref)
    scale = mask_ref[0, LEVELS - 1].astype(F32) * factor(LEVELS - 1)
    alpha = alpha_ref[...] * scale
    copy.wait()
    total = base_ref[...]
    for t in range(SW // 128):
        total = total + q_ref[:, t * 128 : (t + 1) * 128] * alpha[:, t * 128 : (t + 1) * 128]
    row = dot(jnp.ones((8, 128), F32), total, NT)
    sol_ref[...] = row[0:1]
    per_element = dot(row, onehot)
    mine = (iota((8, ELEMS), 1) >> 4) == iota((8, ELEMS), 0)
    spread = mark((iota((ELEMS, NZ), 0) & (EZ - 1)) == (iota((ELEMS, NZ), 1) >> 3))
    rows = dot(jnp.where(mine, per_element, 0.0), spread)
    for a in range(EX):
        add = jnp.broadcast_to(rows[a * EY : (a + 1) * EY, None, :], (EY, NP, NZ)).reshape(NY, NZ)
        for i in range(NP):
            out_ref[a * NP + i] = local_ref[a * NP + i] + add


LZ = EZ * PTS
LXY = PTS * EY * PTS


def local_kernel(
    lam_ref, r_ref, zlow_ref, zhigh_ref, xlow_ref, xhigh_ref, vec_ref, scale_ref, out_ref
):
    lane = iota((NZ + 8, LZ), 1)
    z = iota((NZ + 8, LZ), 0)
    c, p = div_mod(lane, PTS)
    z = jnp.where(z < NZ, z, jnp.where(z == NZ, -1, jnp.where(z == NZ + 1, NZ, -1000)))
    place = z - NP * c + 1
    _, p10 = div_mod(iota((PTS, LZ), 1), PTS)
    repeat = mark(p10 == iota((PTS, LZ), 0))
    v2 = dot(vec_ref[2], repeat)
    bz = jnp.zeros((NZ + 8, LZ), F32)
    for k in range(PTS):
        bz = jnp.where(place == k, v2[k : k + 1, :], bz)
    bz_in = jnp.where((place >= 1) & (place <= NP), bz, 0.0)[0:NZ]
    bz = split(bz)
    bz_in = split(bz_in)

    mb, n = div_mod(iota((PTS, LXY), 1), PTS)
    m, _ = div_mod(iota((PTS, LXY), 1), PTS * EY)
    at = iota((PTS, LXY), 0)
    v1 = dot(vec_ref[1], mark(n == at))
    v0 = dot(vec_ref[0], mark(m == at))
    mb, _ = div_mod(iota((NY, LXY), 1), PTS)
    b = mb & (EY - 1)
    y = iota((NY, LXY), 0)
    place = y - NP * b + 1
    by = jnp.zeros((NY, LXY), F32)
    for j in range(PTS):
        by = jnp.where(place == j, v1[j : j + 1, :], by)
    by_in = jnp.where((place >= 1) & (place <= NP), by, 0.0)
    forward = jnp.concatenate([by * v0[i : i + 1, :] for i in range(PTS)], axis=0)
    forward = split(forward.T)
    back = split(jnp.concatenate([by_in * v0[i : i + 1, :] for i in range(1, NP + 1)], axis=0))

    row = iota((8, NX * NY), 0)
    sides = jnp.where(row == 0, zlow_ref[...], jnp.where(row == 1, zhigh_ref[...], 0.0)).T
    corner_low = xlow_ref[NY : NY + 8, :].T[0:NY]
    corner_high = xhigh_ref[NY : NY + 8, :].T[0:NY]
    sides = jnp.concatenate([corner_low, sides, corner_high], axis=0)
    points = jnp.concatenate(
        [xlow_ref[0:NY, :], r_ref[...].reshape(NX * NY, NZ), xhigh_ref[0:NY, :]], axis=0
    )
    points = jnp.concatenate([points, sides], axis=1)
    section = split(dot3(split(points), bz))

    rows40, lanes160 = EY * PTS, LZ
    rb, rn = div_mod(iota((rows40, EY), 0), PTS)
    pick_b = mark(rb == iota((rows40, EY), 1))
    lc, lp = div_mod(iota((EZ, lanes160), 1), PTS)
    pick_c = mark(lc == iota((EZ, lanes160), 0))
    _, rn = div_mod(iota((rows40, lanes160), 0), PTS)
    _, lp = div_mod(iota((rows40, lanes160), 1), PTS)
    lam = jnp.zeros((rows40, lanes160), F32)
    lam2 = jnp.zeros((rows40, lanes160), F32)
    for k in range(PTS):
        lam = jnp.where(rn == k, lam_ref[1, k], lam)
        lam2 = jnp.where(lp == k, lam_ref[2, k], lam2)
    for a in range(EX):
        factors = dot(dot(pick_b, scale_ref[a]), pick_c)
        window = tuple(s[a * NP * NY : (a * NP + PTS) * NY] for s in section)
        hat = dot3(forward, window)
        scaled = []
        for i in range(PTS):
            denom = factors * ((lam_ref[0, i] + lam) + lam2)
            scaled.append(hat[i * rows40 : (i + 1) * rows40] / denom)
        scaled = jnp.concatenate(scaled, axis=0)
        inner = dot3(back, split(scaled))
        result = dot3(split(inner), bz_in, NT)
        out_ref[a * NP : (a + 1) * NP] = result.reshape(NP, NY, NZ)


def shape(*dims):
    return jax.ShapeDtypeStruct(dims, F32)


def cost(flops, size):
    return pl.CostEstimate(flops=flops, bytes_accessed=size, transcendentals=0)


def per_device(
    residual,
    eigen_vectors,
    eigen_values,
    element_scale,
    vertex_map,
    leaf_columns,
    separator_columns,
    separator_mask,
):
    face_low, face_high = pl.pallas_call(
        face_kernel,
        out_shape=(shape(1, NX * NY), shape(1, NX * NY)),
        in_specs=[VMEM],
        out_specs=(VMEM, VMEM),
        compiler_params=PARAMS,
        name="faces",
    )(residual)
    z_count = lax.axis_size("gz")
    x_count = lax.axis_size("xy")
    up = lambda count: [(i, i + 1) for i in range(count - 1)]
    down = lambda count: [(i + 1, i) for i in range(count - 1)]
    z_low = lax.ppermute(face_high, "gz", up(z_count))
    z_high = lax.ppermute(face_low, "gz", down(z_count))

    partial, b = pl.pallas_call(
        partial_kernel,
        out_shape=(shape(LEVELS, SW), shape(VERTS, 128)),
        in_specs=[VMEM, VMEM, SMEM, ANY],
        out_specs=(VMEM, VMEM),
        scratch_shapes=[
            pltpu.VMEM((VERTS, LEVELS * SW), F32),
            pltpu.SemaphoreType.DMA((CHUNKS,)),
        ],
        compiler_params=PARAMS,
        cost_estimate=cost(6 * 512 * 512 * 2, 7_000_000),
        name="partials",
    )(residual, vertex_map, separator_mask, separator_columns)

    edge_low, edge_high = pl.pallas_call(
        edge_kernel,
        out_shape=(shape(NY + 8, NZ), shape(NY + 8, NZ)),
        in_specs=[VMEM] * 3,
        out_specs=(VMEM, VMEM),
        compiler_params=PARAMS,
        name="edges",
    )(residual, z_low, z_high)
    x_low = lax.ppermute(edge_high, "xy", up(x_count))
    x_high = lax.ppermute(edge_low, "xy", down(x_count))

    level = jnp.arange(LEVELS, dtype=jnp.int32)[:, None]

    def swap(value, axis, bits):
        count = lax.axis_size(axis)
        return lax.ppermute(value, axis, [(i, i ^ bits) for i in range(count)])

    def from_level(value, first):
        return jnp.where(level >= first, value, 0.0)

    total = partial
    one, two, three = (swap(total, "xy", bits) for bits in (1, 2, 3))
    total = total + one + from_level(two + three, 1)
    total = total + from_level(swap(total, "xy", 6), 2)
    one, two, three = (swap(total, "xy", bits) for bits in (8, 16, 24))
    total = total + from_level(one, 3) + from_level(two + three, 4)
    last = total[LEVELS - 1 :]
    last = last + swap(last, "gz", 1)
    last = last + (swap(last, "gz", 2) + swap(last, "gz", 4) + swap(last, "gz", 6))

    local = pl.pallas_call(
        local_kernel,
        out_shape=shape(NX, NY, NZ),
        in_specs=[SMEM] + [VMEM] * 7,
        out_specs=VMEM,
        compiler_params=PARAMS,
        cost_estimate=cost(4_000_000_000, 1_000_000),
        name="local",
    )(eigen_values, residual, z_low, z_high, x_low, x_high, eigen_vectors, element_scale)

    base = pl.pallas_call(
        middle_kernel,
        out_shape=shape(VERTS, 128),
        in_specs=[SMEM, VMEM, VMEM, VMEM, ANY],
        out_specs=VMEM,
        scratch_shapes=[
            pltpu.VMEM((VERTS, (LEVELS - 1) * SW), F32),
            pltpu.SemaphoreType.DMA((CHUNKS,)),
        ],
        compiler_params=PARAMS,
        cost_estimate=cost(7 * 512 * 512 * 2, 7_000_000),
        name="middle",
    )(separator_mask, total, b, leaf_columns, separator_columns)

    out, sol = pl.pallas_call(
        final_kernel,
        out_shape=(shape(NX, NY, NZ), shape(1, VERTS)),
        in_specs=[SMEM, VMEM, VMEM, VMEM, VMEM, ANY],
        out_specs=(VMEM, VMEM),
        scratch_shapes=[pltpu.VMEM((VERTS, SW), F32), pltpu.SemaphoreType.DMA((1,))],
        compiler_params=PARAMS,
        cost_estimate=cost(512 * 512 * 2, 1_500_000),
        name="final",
    )(separator_mask, last, base, local, vertex_map, separator_columns)
    return out, sol.reshape(VERTS)


def solution(mesh):
    placed = (
        P("xy", None, "gz"),
        P(),
        P(),
        P("xy", None, "gz"),
        P("xy", None, "gz"),
        P(("gz", "xy"), None),
        P(("gz", "xy"), None),
        P(("gz", "xy"), None),
    )
    return jax.shard_map(
        per_device,
        mesh=mesh,
        in_specs=placed,
        out_specs=(P("xy", None, "gz"), P(("gz", "xy"))),
        check_vma=False,
    )
```

```python
import functools

import jax
import jax.numpy as jnp
from jax import lax
from jax.experimental import pallas as pl
from jax.experimental.pallas import tpu as pltpu
from jax.sharding import PartitionSpec as P

NP = 8
LEVELS = 6
EX, EY, EZ = 2, 4, 16
VERTS = 512
SW = 512
ELEMS = EX * EY * EZ
NX, NY, NZ = EX * NP, EY * NP, EZ * NP
PTS = NP + 2
CHUNKS = 8
ROWS = VERTS // CHUNKS

F32 = jnp.float32
BF16 = jnp.bfloat16
HIGH = lax.Precision.HIGHEST
VMEM = pl.BlockSpec(memory_space=pltpu.VMEM)
SMEM = pl.BlockSpec(memory_space=pltpu.SMEM)
ANY = pl.BlockSpec(memory_space=pl.ANY)
FIRST_LIMIT = 40 * 2**20
PARAMS = pltpu.CompilerParams(vmem_limit_bytes=40 * 1024 * 1024)
NN = (((1,), (0,)), ((), ()))
NT = (((1,), (1,)), ((), ()))


def dot(a, b, dims=NN):
    return lax.dot_general(a, b, dims, precision=HIGH, preferred_element_type=F32)


def bdot(a, b, dims=NN):
    return lax.dot_general(a, b, dims, preferred_element_type=F32)


def split(a):
    hi = a.astype(BF16)
    return hi, (a - hi.astype(F32)).astype(BF16)


def dot3(a, b, dims=NN):
    return bdot(a[0], b[0], dims) + (bdot(a[0], b[1], dims) + bdot(a[1], b[0], dims))


def iota(shape, axis):
    return lax.broadcasted_iota(jnp.int32, shape, axis)


def div_mod(values, by):
    quotient = jnp.floor((values.astype(F32) + 0.5) * (1.0 / by)).astype(jnp.int32)
    return quotient, values - quotient * by


def mark(condition):
    return condition.astype(F32)


def split3(a):
    hi = a.astype(BF16).astype(F32)
    rest = a - hi
    mid = rest.astype(BF16).astype(F32)
    return hi, mid, rest - mid


def dot_onehot(a, onehot):
    parts = jnp.concatenate([*split3(a), jnp.zeros_like(a)], axis=0).astype(BF16)
    out = bdot(parts, onehot.astype(BF16))
    return out[0:8] + (out[8:16] + out[16:24])


def odd(axis):
    return lax.rem(lax.axis_index(axis), 2)


def factor(level):
    group = 256 if level == LEVELS - 1 else 2 ** (level + 1)
    return float(group) ** (-0.25)


def vertex_values(vm_row, row):
    out = []
    for g in range(VERTS // 8):
        vertex = (iota((8, ELEMS), 0) + g * 8).astype(F32)
        out.append(jnp.sum(jnp.where(vertex == vm_row, row, 0.0), axis=1, keepdims=True))
    return out


TILES = SW // 128
FACE = NY + 8
PARTIALS = LEVELS * TILES
LAST = PARTIALS - TILES


def first_kernel(
    r_hbm, vm_hbm, mask_hbm, q_hbm, vec_hbm, lam_hbm, scale_hbm,
    face_a_ref, face_b_ref, out_ref, aux_ref, r_ref, q_ref, vec_ref, lam_ref, scale_ref,
    v_ref, m_ref, b_ref, sem,
):
    moves = (
        (r_hbm, r_ref), (vm_hbm, v_ref), (mask_hbm, m_ref),
        (vec_hbm, vec_ref), (lam_hbm, lam_ref), (scale_hbm, scale_ref),
    )
    small = [
        pltpu.make_async_copy(src, dst, sem.at[CHUNKS + i]) for i, (src, dst) in enumerate(moves)
    ]
    for copy in small:
        copy.start()
    large = []
    for c in range(CHUNKS):
        rows = pl.ds(c * ROWS, ROWS)
        large.append(pltpu.make_async_copy(q_hbm.at[rows], q_ref.at[rows], sem.at[c]))
        large[-1].start()
    small[1].wait()
    vm = jnp.concatenate([v_ref[0], v_ref[1]], axis=0).astype(F32)
    mine = (iota((8, ELEMS), 1) >> 4) == iota((8, ELEMS), 0)
    spread = mark(iota((EZ, ELEMS), 0) == (iota((EZ, ELEMS), 1) & (EZ - 1)))
    vm_row = jnp.sum(jnp.where(mine, dot_onehot(vm, spread), 0.0), axis=0, keepdims=True)
    small[2].wait()
    scales = []
    for level in range(LEVELS):
        value = m_ref[0:1, level : level + 1].astype(F32) * factor(level)
        scales.append(jnp.broadcast_to(value, (1, 128)))
        aux_ref[level : level + 1, :] = scales[-1]
    aux_ref[LEVELS : LEVELS + 1, :] = vm_row
    small[0].wait()
    sums = []
    for a in range(EX):
        total = r_ref[a * NP]
        for i in range(1, NP):
            total = total + r_ref[a * NP + i]
        sums.append(jnp.sum(total.reshape(EY, NP, NZ), axis=1))
    sums = jnp.concatenate(sums, axis=0) * (1.0 / NP**3)
    gather = mark((iota((NZ, ELEMS), 0) >> 3) == (iota((NZ, ELEMS), 1) & (EZ - 1)))
    means = jnp.sum(jnp.where(mine, dot_onehot(sums, gather), 0.0), axis=0, keepdims=True)
    aux_ref[LEVELS + 1 : LEVELS + 2, :] = means
    for g, value in enumerate(vertex_values(vm_row, means)):
        b_ref[g * 8 : g * 8 + 8, :] = jnp.broadcast_to(value, (8, 128))
    flat = r_ref[...].reshape(NX * NY, NZ)
    row, lane = iota((8, NZ), 0), iota((8, NZ), 1)
    side = odd("gz")
    lane_a = (1 - side) * (NZ - 1)
    lane_b = side * (NZ - 1)
    pick = mark(((row == 0) & (lane == lane_a)) | ((row == 1) & (lane == lane_b)))
    faces = dot(pick, flat, NT)
    for k in range(4):
        face_a_ref[k : k + 1, :] = faces[0:1, k * 128 : (k + 1) * 128]
        face_b_ref[k : k + 1, :] = faces[1:2, k * 128 : (k + 1) * 128]
    acc = [jnp.zeros((8, 128), F32) for _ in range(PARTIALS)]
    for c in range(CHUNKS):
        large[c].wait()
        for g in range(ROWS // 8):
            at = c * ROWS + g * 8
            b = b_ref[at : at + 8, :]
            for t in range(PARTIALS):
                acc[t] = acc[t] + q_ref[at : at + 8, t * 128 : (t + 1) * 128] * b
    for t in range(PARTIALS):
        total = jnp.sum(acc[t], axis=0, keepdims=True) * scales[t // TILES]
        out_ref[t : t + 1, :] = total
        if t >= LAST:
            face_a_ref[4 + t - LAST : 5 + t - LAST, :] = total
    for copy in small[3:]:
        copy.wait()


def edge_kernel(r_ref, za_ref, zb_ref, partial_ref, a_ref, b_ref):
    side = odd("gz")
    za, zb = za_ref[0:4, :], zb_ref[...]
    low = jnp.where(side == 1, za, zb)
    high = jnp.where(side == 1, zb, za)
    turned = odd("xy") == 1
    first, last = r_ref[0], r_ref[NX - 1]
    for out, take in ((a_ref, turned), (b_ref, jnp.logical_not(turned))):
        out[0:NY, :] = jnp.where(take, first, last)
        out[NY:FACE, :] = jnp.zeros((8, NZ), F32)
        for i, edge in enumerate((low, high)):
            out[NY + i : NY + i + 1, 0:NY] = jnp.where(take, edge[0:1, 0:NY], edge[3:4, 128 - NY :])
    a_ref[FACE : FACE + PARTIALS, :] = partial_ref[...]


def middle_kernel(scale_ref, alpha_ref, leaf_ref, q_ref, out_ref):
    acc = [jnp.zeros((8, 128), F32) for _ in range(TILES)]
    values = vertex_values(scale_ref[LEVELS : LEVELS + 1, :], scale_ref[LEVELS + 1 : LEVELS + 2, :])
    for g, b in enumerate(values):
        for t in range(TILES):
            acc[t] = acc[t] + leaf_ref[g * 8 : g * 8 + 8, t * 128 : (t + 1) * 128] * b
    leaf_alpha = [jnp.sum(acc[t], axis=0, keepdims=True) for t in range(TILES)]
    alpha = []
    for t in range((LEVELS - 1) * TILES):
        level = t // TILES
        alpha.append(alpha_ref[t : t + 1, :] * scale_ref[level : level + 1, :])
    for c in range(CHUNKS):
        rows = slice(c * ROWS, (c + 1) * ROWS)
        total = leaf_ref[rows, 0:128] * leaf_alpha[0]
        for t in range(1, TILES):
            total = total + leaf_ref[rows, t * 128 : (t + 1) * 128] * leaf_alpha[t]
        for t in range(len(alpha)):
            total = total + q_ref[rows, t * 128 : (t + 1) * 128] * alpha[t]
        out_ref[rows, :] = total


def final_kernel(scale_ref, alpha_ref, base_ref, low_ref, high_ref, q_ref, out_ref, sol_ref):
    alpha = alpha_ref[...] * scale_ref[LEVELS - 1 : LEVELS, :]
    start = (LEVELS - 1) * SW
    vm_row = scale_ref[LEVELS : LEVELS + 1, :]
    acc = jnp.zeros((8, ELEMS), F32)
    totals = []
    for g in range(VERTS // 8):
        rows = slice(g * 8, g * 8 + 8)
        total = base_ref[rows, :]
        for t in range(TILES):
            at = start + t * 128
            total = total + q_ref[rows, at : at + 128] * alpha[t : t + 1, :]
        totals.append(total)
        value = jnp.sum(total, axis=1, keepdims=True)
        vertex = (iota((8, ELEMS), 0) + g * 8).astype(F32)
        acc = acc + jnp.where(vertex == vm_row, value, 0.0)
    per_element = jnp.sum(acc, axis=0, keepdims=True)
    mine = (iota((8, ELEMS), 1) >> 4) == iota((8, ELEMS), 0)
    spread = mark((iota((ELEMS, NZ), 0) & (EZ - 1)) == (iota((ELEMS, NZ), 1) >> 3))
    rows = dot_onehot(jnp.where(mine, per_element, 0.0), spread)
    for a, local_ref in enumerate((low_ref, high_ref)):
        add = jnp.broadcast_to(rows[a * EY : (a + 1) * EY, None, :], (EY, NP, NZ)).reshape(NY, NZ)
        for i in range(NP):
            out_ref[a * NP + i] = local_ref[i] + add
    ones = jnp.ones((8, 128), BF16)
    row = [bdot(ones, part.astype(BF16), NT) for part in split3(jnp.concatenate(totals, axis=0))]
    sol_ref[...] = (row[0] + (row[1] + row[2]))[0:1]


LZ = EZ * PTS
LXY = PTS * EY * PTS


def prep_kernel(
    lam_ref, vec_ref, scale_ref, bz0_ref, bz1_ref, in0_ref, in1_ref, f0_ref, f1_ref, k0_ref, k1_ref, inv_ref
):
    lane = iota((NZ + 8, LZ), 1)
    z = iota((NZ + 8, LZ), 0)
    c, p = div_mod(lane, PTS)
    z = jnp.where(z < NZ, z, jnp.where(z == NZ, -1, jnp.where(z == NZ + 1, NZ, -1000)))
    place = z - NP * c + 1
    _, p10 = div_mod(iota((PTS, LZ), 1), PTS)
    repeat = mark(p10 == iota((PTS, LZ), 0))
    v2 = dot(vec_ref[:, 2, :], repeat)
    bz = jnp.zeros((NZ + 8, LZ), F32)
    for k in range(PTS):
        bz = jnp.where(place == k, v2[k : k + 1, :], bz)
    bz_in = jnp.where((place >= 1) & (place <= NP), bz, 0.0)[0:NZ]
    bz0_ref[...], bz1_ref[...] = split(bz)
    in0_ref[...], in1_ref[...] = split(bz_in)

    _, n = div_mod(iota((PTS, LXY), 1), PTS)
    m, _ = div_mod(iota((PTS, LXY), 1), PTS * EY)
    at = iota((PTS, LXY), 0)
    v1 = dot(vec_ref[:, 1, :], mark(n == at))
    v0 = dot(vec_ref[:, 0, :], mark(m == at))
    mb, _ = div_mod(iota((NY, LXY), 1), PTS)
    b = mb & (EY - 1)
    y = iota((NY, LXY), 0)
    place = y - NP * b + 1
    by = jnp.zeros((NY, LXY), F32)
    for j in range(PTS):
        by = jnp.where(place == j, v1[j : j + 1, :], by)
    by_in = jnp.where((place >= 1) & (place <= NP), by, 0.0)
    forward = jnp.concatenate([by * v0[i : i + 1, :] for i in range(PTS)], axis=0)
    f0_ref[...], f1_ref[...] = split(forward.T)
    back = jnp.concatenate([by_in * v0[i : i + 1, :] for i in range(1, NP + 1)], axis=0)
    k0_ref[...], k1_ref[...] = split(back)

    rows40 = EY * PTS
    rb, _ = div_mod(iota((rows40, EY), 0), PTS)
    pick_b = mark(rb == iota((rows40, EY), 1))
    lc, _ = div_mod(iota((EZ, LZ), 1), PTS)
    pick_c = mark(lc == iota((EZ, LZ), 0))
    _, rn = div_mod(iota((rows40, LZ), 0), PTS)
    _, lp = div_mod(iota((rows40, LZ), 1), PTS)
    lam = jnp.zeros((rows40, LZ), F32)
    lam2 = jnp.zeros((rows40, LZ), F32)
    for k in range(PTS):
        lam = jnp.where(rn == k, lam_ref[1:2, k : k + 1], lam)
        lam2 = jnp.where(lp == k, lam_ref[2:3, k : k + 1], lam2)
    for a in range(EX):
        factors = dot(dot(pick_b, scale_ref[a]), pick_c)
        for i in range(PTS):
            inv_ref[a, i * rows40 : (i + 1) * rows40, :] = 1.0 / (
                factors * ((lam_ref[0:1, i : i + 1] + lam) + lam2)
            )


def local_kernel(
    a, r_ref, za_ref, zb_ref, xa_ref, xb_ref,
    bz0_ref, bz1_ref, in0_ref, in1_ref, f0_ref, f1_ref, k0_ref, k1_ref, inv_ref, out_ref,
):
    row = iota((8, 128), 0)
    side = odd("gz")
    za, zb = za_ref[0:4, :], zb_ref[...]
    zlow, zhigh = jnp.where(side == 1, za, zb), jnp.where(side == 1, zb, za)
    turned = odd("xy") == 1
    xa, xb = xa_ref[0:FACE, :], xb_ref[...]
    xlow, xhigh = jnp.where(turned, xa, xb), jnp.where(turned, xb, xa)
    sides = [
        jnp.where(row == 0, zlow[k : k + 1], jnp.where(row == 1, zhigh[k : k + 1], 0.0)).T
        for k in range(4)
    ]
    sides = jnp.concatenate([xlow[NY:FACE].T[0:NY], *sides, xhigh[NY:FACE].T[0:NY]], axis=0)
    points = jnp.concatenate([xlow[0:NY], r_ref[...].reshape(NX * NY, NZ), xhigh[0:NY]], axis=0)
    points = jnp.concatenate([points, sides], axis=1)[a * NP * NY : (a * NP + PTS) * NY]
    window = split(dot3(split(points), (bz0_ref[...], bz1_ref[...])))
    scaled = dot3((f0_ref[...], f1_ref[...]), window) * inv_ref[a]
    inner = dot3((k0_ref[...], k1_ref[...]), split(scaled))
    result = dot3(split(inner), (in0_ref[...], in1_ref[...]), NT)
    out_ref[...] = result.reshape(NP, NY, NZ)


def shape(*dims):
    return jax.ShapeDtypeStruct(dims, F32)


def cost(flops, size):
    return pl.CostEstimate(flops=flops, bytes_accessed=size, transcendentals=0)


def per_device(
    residual,
    eigen_vectors,
    eigen_values,
    element_scale,
    vertex_map,
    leaf_columns,
    separator_columns,
    separator_mask,
):
    face_a, face_b, partial, aux, points, separators, vectors, values, scale = pl.pallas_call(
        first_kernel,
        out_shape=(
            shape(8, 128), shape(4, 128), shape(PARTIALS, 128), shape(8, 128),
            shape(NX, NY, NZ), shape(VERTS, LEVELS * SW),
            shape(PTS, 3, PTS), shape(3, PTS), shape(EX, EY, EZ),
        ),
        in_specs=[pl.BlockSpec(memory_space=pltpu.HBM)] * 7,
        out_specs=(VMEM,) * 9,
        scratch_shapes=[
            pltpu.VMEM((EX, EY, EZ), jnp.int32),
            pltpu.VMEM((1, LEVELS), jnp.int32),
            pltpu.VMEM((VERTS, 128), F32),
            pltpu.SemaphoreType.DMA((CHUNKS + 6,)),
        ],
        compiler_params=pltpu.CompilerParams(vmem_limit_bytes=FIRST_LIMIT),
        cost_estimate=cost(6 * 512 * 512 * 2, 6_500_000),
        name="first",
    )(
        *(
            pltpu.with_memory_space_constraint(x, pltpu.HBM)
            for x in (
                residual, vertex_map, separator_mask, separator_columns,
                eigen_vectors.transpose(1, 0, 2), eigen_values, element_scale,
            )
        )
    )

    def swap(value, axis, bits):
        return lax.ppermute(value, axis, [(i, i ^ bits) for i in range(lax.axis_size(axis))])

    def pairs(value, axis):
        odds = range(1, lax.axis_size(axis) - 1, 2)
        return lax.ppermute(value, axis, [p for i in odds for p in ((i, i + 1), (i + 1, i))])

    z_a = swap(face_a, "gz", 1)
    z_b = pairs(face_b, "gz")

    last = partial[LAST:] + z_a[4:]
    total = jnp.concatenate([partial[:LAST], last], axis=0)

    message_a, message_b = pl.pallas_call(
        edge_kernel,
        out_shape=(shape(FACE + PARTIALS, NZ), shape(FACE, NZ)),
        in_specs=[VMEM] * 4,
        out_specs=(VMEM, VMEM),
        compiler_params=PARAMS,
        cost_estimate=cost(1000, 100_000),
        name="edges",
    )(points, z_a, z_b, total)

    level = jnp.arange(PARTIALS, dtype=jnp.int32)[:, None] // TILES

    def from_level(value, first):
        return jnp.where(level >= first, value, 0.0)

    two, three = swap(total, "xy", 2), swap(total, "xy", 3)
    x_a = swap(message_a, "xy", 1)
    x_b = pairs(message_b, "xy")
    total = total + x_a[FACE:] + from_level(two + three, 1)
    total, x_b = lax.optimization_barrier((total, x_b))
    total = total + from_level(swap(total, "xy", 6), 2)
    half = lambda *dims: jax.ShapeDtypeStruct(dims, BF16)
    matrices = pl.pallas_call(
        prep_kernel,
        out_shape=(half(NZ + 8, LZ),) * 2
        + (half(NZ, LZ),) * 2
        + (half(LXY, PTS * NY),) * 2
        + (half(NP * NY, LXY),) * 2
        + (shape(EX, LXY, LZ),),
        in_specs=[VMEM] * 3,
        out_specs=(VMEM,) * 9,
        compiler_params=PARAMS,
        cost_estimate=cost(1_000_000_000, 1_000_000),
        name="prep",
    )(values, vectors, scale)
    total, matrices = lax.optimization_barrier((total, matrices))
    one, two, three = (swap(total, "xy", bits) for bits in (8, 16, 24))
    total = total + from_level(one, 3) + from_level(two + three, 4)

    def local(a):
        return pl.pallas_call(
            functools.partial(local_kernel, a),
            out_shape=shape(NP, NY, NZ),
            in_specs=[VMEM] * 14,
            out_specs=VMEM,
            compiler_params=PARAMS,
            cost_estimate=cost(1_000_000_000, 1_000_000),
            name="local",
        )(points, z_a, z_b, x_a, x_b, *matrices)

    low = local(0)
    total, low = lax.optimization_barrier((total, low))
    last = total[LAST:]
    last = last + (swap(last, "gz", 2) + swap(last, "gz", 4) + swap(last, "gz", 6))
    high = local(1)
    base = pl.pallas_call(
        middle_kernel,
        out_shape=shape(VERTS, 128),
        in_specs=[VMEM] * 4,
        out_specs=VMEM,
        compiler_params=PARAMS,
        cost_estimate=cost(7 * 512 * 512 * 2, 7_000_000),
        name="middle",
    )(aux, total, leaf_columns, separators)

    out, sol = pl.pallas_call(
        final_kernel,
        out_shape=(shape(NX, NY, NZ), shape(1, VERTS)),
        in_specs=[VMEM] * 6,
        out_specs=(VMEM, VMEM),
        compiler_params=PARAMS,
        cost_estimate=cost(512 * 512 * 2, 1_500_000),
        name="final",
    )(aux, last, base, low, high, separators)
    return out, sol.reshape(VERTS)


def solution(mesh):
    placed = (
        P("xy", None, "gz"),
        P(),
        P(),
        P("xy", None, "gz"),
        P("xy", None, "gz"),
        P(("gz", "xy"), None),
        P(("gz", "xy"), None),
        P(("gz", "xy"), None),
    )
    return jax.shard_map(
        per_device,
        mesh=mesh,
        in_specs=placed,
        out_specs=(P("xy", None, "gz"), P(("gz", "xy"))),
        check_vma=False,
    )
```

```python
import functools

import jax
import jax.numpy as jnp
from jax import lax
from jax.experimental import pallas as pl
from jax.experimental.pallas import tpu as pltpu
from jax.sharding import PartitionSpec as P

NP = 8
LEVELS = 6
EX, EY, EZ = 2, 4, 16
VERTS = 512
SW = 512
ELEMS = EX * EY * EZ
NX, NY, NZ = EX * NP, EY * NP, EZ * NP
PTS = NP + 2
CHUNKS = 8
ROWS = VERTS // CHUNKS

F32 = jnp.float32
BF16 = jnp.bfloat16
HIGH = lax.Precision.HIGHEST
VMEM = pl.BlockSpec(memory_space=pltpu.VMEM)
SMEM = pl.BlockSpec(memory_space=pltpu.SMEM)
ANY = pl.BlockSpec(memory_space=pl.ANY)
FIRST_LIMIT = 40 * 2**20
PARAMS = pltpu.CompilerParams(vmem_limit_bytes=40 * 1024 * 1024)
NN = (((1,), (0,)), ((), ()))
NT = (((1,), (1,)), ((), ()))


def dot(a, b, dims=NN):
    return lax.dot_general(a, b, dims, precision=HIGH, preferred_element_type=F32)


def bdot(a, b, dims=NN):
    return lax.dot_general(a, b, dims, preferred_element_type=F32)


def split(a):
    hi = a.astype(BF16)
    return hi, (a - hi.astype(F32)).astype(BF16)


def dot3(a, b, dims=NN):
    return bdot(a[0], b[0], dims) + (bdot(a[0], b[1], dims) + bdot(a[1], b[0], dims))


def iota(shape, axis):
    return lax.broadcasted_iota(jnp.int32, shape, axis)


def div_mod(values, by):
    quotient = jnp.floor((values.astype(F32) + 0.5) * (1.0 / by)).astype(jnp.int32)
    return quotient, values - quotient * by


def mark(condition):
    return condition.astype(F32)


def split3(a):
    hi = a.astype(BF16).astype(F32)
    rest = a - hi
    mid = rest.astype(BF16).astype(F32)
    return hi, mid, rest - mid


def dot_onehot(a, onehot):
    parts = jnp.concatenate([*split3(a), jnp.zeros_like(a)], axis=0).astype(BF16)
    out = bdot(parts, onehot.astype(BF16))
    return out[0:8] + (out[8:16] + out[16:24])


def odd(axis):
    return lax.rem(lax.axis_index(axis), 2)


def inside(axis, value):
    at = lax.axis_index(axis)
    return jnp.where((at > 0) & (at < lax.axis_size(axis) - 1), value, 0.0)


def factor(level):
    group = 256 if level == LEVELS - 1 else 2 ** (level + 1)
    return float(group) ** (-0.25)


def vertex_values(vm_row, row):
    out = []
    for g in range(VERTS // 8):
        vertex = (iota((8, ELEMS), 0) + g * 8).astype(F32)
        out.append(jnp.sum(jnp.where(vertex == vm_row, row, 0.0), axis=1, keepdims=True))
    return out


TILES = SW // 128
FACE = NY + 8
PARTIALS = LEVELS * TILES
LAST = PARTIALS - TILES


def first_kernel(
    r_hbm, vm_hbm, mask_hbm, q_hbm, vec_hbm, lam_hbm, scale_hbm,
    face_a_ref, face_b_ref, out_ref, aux_ref, r_ref, q_ref, vec_ref, lam_ref, scale_ref,
    v_ref, m_ref, b_ref, sem,
):
    moves = (
        (r_hbm, r_ref), (vm_hbm, v_ref), (mask_hbm, m_ref),
        (vec_hbm, vec_ref), (lam_hbm, lam_ref), (scale_hbm, scale_ref),
    )
    small = [
        pltpu.make_async_copy(src, dst, sem.at[CHUNKS + i]) for i, (src, dst) in enumerate(moves)
    ]
    for copy in small:
        copy.start()
    large = []
    for c in range(CHUNKS):
        rows = pl.ds(c * ROWS, ROWS)
        large.append(pltpu.make_async_copy(q_hbm.at[rows], q_ref.at[rows], sem.at[c]))
        large[-1].start()
    small[1].wait()
    vm = jnp.concatenate([v_ref[0], v_ref[1]], axis=0).astype(F32)
    mine = (iota((8, ELEMS), 1) >> 4) == iota((8, ELEMS), 0)
    spread = mark(iota((EZ, ELEMS), 0) == (iota((EZ, ELEMS), 1) & (EZ - 1)))
    vm_row = jnp.sum(jnp.where(mine, dot_onehot(vm, spread), 0.0), axis=0, keepdims=True)
    small[2].wait()
    scales = []
    for level in range(LEVELS):
        value = m_ref[0:1, level : level + 1].astype(F32) * factor(level)
        scales.append(jnp.broadcast_to(value, (1, 128)))
        aux_ref[level : level + 1, :] = scales[-1]
    aux_ref[LEVELS : LEVELS + 1, :] = vm_row
    small[0].wait()
    sums = []
    for a in range(EX):
        total = r_ref[a * NP]
        for i in range(1, NP):
            total = total + r_ref[a * NP + i]
        sums.append(jnp.sum(total.reshape(EY, NP, NZ), axis=1))
    sums = jnp.concatenate(sums, axis=0) * (1.0 / NP**3)
    gather = mark((iota((NZ, ELEMS), 0) >> 3) == (iota((NZ, ELEMS), 1) & (EZ - 1)))
    means = jnp.sum(jnp.where(mine, dot_onehot(sums, gather), 0.0), axis=0, keepdims=True)
    aux_ref[LEVELS + 1 : LEVELS + 2, :] = means
    for g, value in enumerate(vertex_values(vm_row, means)):
        b_ref[g * 8 : g * 8 + 8, :] = jnp.broadcast_to(value, (8, 128))
    flat = r_ref[...].reshape(NX * NY, NZ)
    row, lane = iota((8, NZ), 0), iota((8, NZ), 1)
    side = odd("gz")
    lane_a = (1 - side) * (NZ - 1)
    lane_b = side * (NZ - 1)
    pick = mark(((row == 0) & (lane == lane_a)) | ((row == 1) & (lane == lane_b)))
    faces = dot(pick, flat, NT)
    for k in range(4):
        face_a_ref[k : k + 1, :] = faces[0:1, k * 128 : (k + 1) * 128]
        face_b_ref[k : k + 1, :] = faces[1:2, k * 128 : (k + 1) * 128]
    acc = [jnp.zeros((8, 128), F32) for _ in range(PARTIALS)]
    for c in range(CHUNKS):
        large[c].wait()
        for g in range(ROWS // 8):
            at = c * ROWS + g * 8
            b = b_ref[at : at + 8, :]
            for t in range(PARTIALS):
                acc[t] = acc[t] + q_ref[at : at + 8, t * 128 : (t + 1) * 128] * b
    for t in range(PARTIALS):
        total = jnp.sum(acc[t], axis=0, keepdims=True) * scales[t // TILES]
        out_ref[t : t + 1, :] = total
        if t >= LAST:
            face_a_ref[4 + t - LAST : 5 + t - LAST, :] = total
    for copy in small[3:]:
        copy.wait()


def edge_kernel(r_ref, za_ref, zb_ref, partial_ref, a_ref, b_ref):
    side = odd("gz")
    za, zb = za_ref[0:4, :], inside("gz", zb_ref[...])
    low = jnp.where(side == 1, za, zb)
    high = jnp.where(side == 1, zb, za)
    turned = odd("xy") == 1
    first, last = r_ref[0], r_ref[NX - 1]
    for out, take in ((a_ref, turned), (b_ref, jnp.logical_not(turned))):
        out[0:NY, :] = jnp.where(take, first, last)
        out[NY:FACE, :] = jnp.zeros((8, NZ), F32)
        for i, edge in enumerate((low, high)):
            out[NY + i : NY + i + 1, 0:NY] = jnp.where(take, edge[0:1, 0:NY], edge[3:4, 128 - NY :])
    a_ref[FACE : FACE + PARTIALS, :] = partial_ref[...]


def middle_kernel(scale_ref, alpha_ref, leaf_ref, q_ref, out_ref):
    acc = [jnp.zeros((8, 128), F32) for _ in range(TILES)]
    values = vertex_values(scale_ref[LEVELS : LEVELS + 1, :], scale_ref[LEVELS + 1 : LEVELS + 2, :])
    for g, b in enumerate(values):
        for t in range(TILES):
            acc[t] = acc[t] + leaf_ref[g * 8 : g * 8 + 8, t * 128 : (t + 1) * 128] * b
    leaf_alpha = [jnp.sum(acc[t], axis=0, keepdims=True) for t in range(TILES)]
    alpha = []
    for t in range((LEVELS - 1) * TILES):
        level = t // TILES
        alpha.append(alpha_ref[t : t + 1, :] * scale_ref[level : level + 1, :])
    for c in range(CHUNKS):
        rows = slice(c * ROWS, (c + 1) * ROWS)
        total = leaf_ref[rows, 0:128] * leaf_alpha[0]
        for t in range(1, TILES):
            total = total + leaf_ref[rows, t * 128 : (t + 1) * 128] * leaf_alpha[t]
        for t in range(len(alpha)):
            total = total + q_ref[rows, t * 128 : (t + 1) * 128] * alpha[t]
        out_ref[rows, :] = total


def final_kernel(scale_ref, alpha_ref, base_ref, near_ref, far_ref, q_ref, out_ref, sol_ref):
    alpha = alpha_ref[...] * scale_ref[LEVELS - 1 : LEVELS, :]
    start = (LEVELS - 1) * SW
    vm_row = scale_ref[LEVELS : LEVELS + 1, :]
    acc = jnp.zeros((8, ELEMS), F32)
    totals = []
    for g in range(VERTS // 8):
        rows = slice(g * 8, g * 8 + 8)
        total = base_ref[rows, :]
        for t in range(TILES):
            at = start + t * 128
            total = total + q_ref[rows, at : at + 128] * alpha[t : t + 1, :]
        totals.append(total)
        value = jnp.sum(total, axis=1, keepdims=True)
        vertex = (iota((8, ELEMS), 0) + g * 8).astype(F32)
        acc = acc + jnp.where(vertex == vm_row, value, 0.0)
    per_element = jnp.sum(acc, axis=0, keepdims=True)
    mine = (iota((8, ELEMS), 1) >> 4) == iota((8, ELEMS), 0)
    spread = mark((iota((ELEMS, NZ), 0) & (EZ - 1)) == (iota((ELEMS, NZ), 1) >> 3))
    rows = dot_onehot(jnp.where(mine, per_element, 0.0), spread)
    turned = odd("xy") == 1
    for a in range(EX):
        add = jnp.broadcast_to(rows[a * EY : (a + 1) * EY, None, :], (EY, NP, NZ)).reshape(NY, NZ)
        for i in range(NP):
            local = jnp.where(turned == (a == 0), near_ref[i], far_ref[i])
            out_ref[a * NP + i] = local + add
    ones = jnp.ones((8, 128), BF16)
    row = [bdot(ones, part.astype(BF16), NT) for part in split3(jnp.concatenate(totals, axis=0))]
    sol_ref[...] = (row[0] + (row[1] + row[2]))[0:1]


LZ = EZ * PTS
LXY = PTS * EY * PTS


def prep_kernel(
    lam_ref, vec_ref, scale_ref, bz0_ref, bz1_ref, in0_ref, in1_ref, f0_ref, f1_ref, k0_ref, k1_ref, inv_ref
):
    lane = iota((NZ + 8, LZ), 1)
    z = iota((NZ + 8, LZ), 0)
    c, p = div_mod(lane, PTS)
    z = jnp.where(z < NZ, z, jnp.where(z == NZ, -1, jnp.where(z == NZ + 1, NZ, -1000)))
    place = z - NP * c + 1
    _, p10 = div_mod(iota((PTS, LZ), 1), PTS)
    repeat = mark(p10 == iota((PTS, LZ), 0))
    v2 = dot(vec_ref[:, 2, :], repeat)
    bz = jnp.zeros((NZ + 8, LZ), F32)
    for k in range(PTS):
        bz = jnp.where(place == k, v2[k : k + 1, :], bz)
    bz_in = jnp.where((place >= 1) & (place <= NP), bz, 0.0)[0:NZ]
    bz0_ref[...], bz1_ref[...] = split(bz)
    in0_ref[...], in1_ref[...] = split(bz_in)

    _, n = div_mod(iota((PTS, LXY), 1), PTS)
    m, _ = div_mod(iota((PTS, LXY), 1), PTS * EY)
    at = iota((PTS, LXY), 0)
    v1 = dot(vec_ref[:, 1, :], mark(n == at))
    v0 = dot(vec_ref[:, 0, :], mark(m == at))
    mb, _ = div_mod(iota((NY, LXY), 1), PTS)
    b = mb & (EY - 1)
    y = iota((NY, LXY), 0)
    place = y - NP * b + 1
    by = jnp.zeros((NY, LXY), F32)
    for j in range(PTS):
        by = jnp.where(place == j, v1[j : j + 1, :], by)
    by_in = jnp.where((place >= 1) & (place <= NP), by, 0.0)
    forward = jnp.concatenate([by * v0[i : i + 1, :] for i in range(PTS)], axis=0)
    f0_ref[...], f1_ref[...] = split(forward.T)
    back = jnp.concatenate([by_in * v0[i : i + 1, :] for i in range(1, NP + 1)], axis=0)
    k0_ref[...], k1_ref[...] = split(back)

    rows40 = EY * PTS
    rb, _ = div_mod(iota((rows40, EY), 0), PTS)
    pick_b = mark(rb == iota((rows40, EY), 1))
    lc, _ = div_mod(iota((EZ, LZ), 1), PTS)
    pick_c = mark(lc == iota((EZ, LZ), 0))
    _, rn = div_mod(iota((rows40, LZ), 0), PTS)
    _, lp = div_mod(iota((rows40, LZ), 1), PTS)
    lam = jnp.zeros((rows40, LZ), F32)
    lam2 = jnp.zeros((rows40, LZ), F32)
    for k in range(PTS):
        lam = jnp.where(rn == k, lam_ref[1:2, k : k + 1], lam)
        lam2 = jnp.where(lp == k, lam_ref[2:3, k : k + 1], lam2)
    for a in range(EX):
        factors = dot(dot(pick_b, scale_ref[a]), pick_c)
        for i in range(PTS):
            inv_ref[a, i * rows40 : (i + 1) * rows40, :] = 1.0 / (
                factors * ((lam_ref[0:1, i : i + 1] + lam) + lam2)
            )


def local_kernel(
    other, r_ref, za_ref, zb_ref, face_ref,
    bz0_ref, bz1_ref, in0_ref, in1_ref, f0_ref, f1_ref, k0_ref, k1_ref, inv_ref, out_ref,
):
    row = iota((8, 128), 0)
    side = odd("gz")
    za, zb = za_ref[0:4, :], inside("gz", zb_ref[...])
    zlow, zhigh = jnp.where(side == 1, za, zb), jnp.where(side == 1, zb, za)
    face = face_ref[0:FACE, :]
    if other:
        face = inside("xy", face)
    at = odd("xy") if other else 1 - odd("xy")
    before = at == 0
    sides = [
        jnp.where(row == 0, zlow[k : k + 1], jnp.where(row == 1, zhigh[k : k + 1], 0.0)).T
        for k in range(4)
    ]
    edge = face[NY:FACE].T[0:NY]
    own = r_ref[pl.ds(at * (NP - 1), NP + 1)].reshape((NP + 1) * NY, NZ)
    sides = jnp.concatenate(sides, axis=0)
    sides = jnp.where(before, sides[: (NP + 1) * NY], sides[(NP - 1) * NY :])
    points = jnp.where(
        before,
        jnp.concatenate([face[0:NY], own], axis=0),
        jnp.concatenate([own, face[0:NY]], axis=0),
    )
    sides = jnp.where(
        before, jnp.concatenate([edge, sides], axis=0), jnp.concatenate([sides, edge], axis=0)
    )
    points = jnp.concatenate([points, sides], axis=1)
    window = split(dot3(split(points), (bz0_ref[...], bz1_ref[...])))
    scaled = dot3((f0_ref[...], f1_ref[...]), window) * inv_ref[at]
    inner = dot3((k0_ref[...], k1_ref[...]), split(scaled))
    result = dot3(split(inner), (in0_ref[...], in1_ref[...]), NT)
    out_ref[...] = result.reshape(NP, NY, NZ)


def shape(*dims):
    return jax.ShapeDtypeStruct(dims, F32)


def cost(flops, size):
    return pl.CostEstimate(flops=flops, bytes_accessed=size, transcendentals=0)


def per_device(
    residual,
    eigen_vectors,
    eigen_values,
    element_scale,
    vertex_map,
    leaf_columns,
    separator_columns,
    separator_mask,
):
    face_a, face_b, partial, aux, points, separators, vectors, values, scale = pl.pallas_call(
        first_kernel,
        out_shape=(
            shape(8, 128), shape(4, 128), shape(PARTIALS, 128), shape(8, 128),
            shape(NX, NY, NZ), shape(VERTS, LEVELS * SW),
            shape(PTS, 3, PTS), shape(3, PTS), shape(EX, EY, EZ),
        ),
        in_specs=[pl.BlockSpec(memory_space=pltpu.HBM)] * 7,
        out_specs=(VMEM,) * 9,
        scratch_shapes=[
            pltpu.VMEM((EX, EY, EZ), jnp.int32),
            pltpu.VMEM((1, LEVELS), jnp.int32),
            pltpu.VMEM((VERTS, 128), F32),
            pltpu.SemaphoreType.DMA((CHUNKS + 6,)),
        ],
        compiler_params=pltpu.CompilerParams(vmem_limit_bytes=FIRST_LIMIT),
        cost_estimate=cost(6 * 512 * 512 * 2, 6_500_000),
        name="first",
    )(
        *(
            pltpu.with_memory_space_constraint(x, pltpu.HBM)
            for x in (
                residual, vertex_map, separator_mask, separator_columns,
                eigen_vectors.transpose(1, 0, 2), eigen_values, element_scale,
            )
        )
    )

    def swap(value, axis, bits):
        return lax.ppermute(value, axis, [(i, i ^ bits) for i in range(lax.axis_size(axis))])

    def pairs(value, axis):
        count = lax.axis_size(axis)
        return lax.ppermute(value, axis, [(i, (i + 2 * (i % 2) - 1) % count) for i in range(count)])

    z_a = swap(face_a, "gz", 1)
    z_b = pairs(face_b, "gz")

    last = partial[LAST:] + z_a[4:]
    total = jnp.concatenate([partial[:LAST], last], axis=0)

    message_a, message_b = pl.pallas_call(
        edge_kernel,
        out_shape=(shape(FACE + PARTIALS, NZ), shape(FACE, NZ)),
        in_specs=[VMEM] * 4,
        out_specs=(VMEM, VMEM),
        compiler_params=PARAMS,
        cost_estimate=cost(1000, 100_000),
        name="edges",
    )(points, z_a, z_b, total)

    level = jnp.arange(PARTIALS, dtype=jnp.int32)[:, None] // TILES

    def from_level(value, first):
        return jnp.where(level >= first, value, 0.0)

    two, three = swap(total, "xy", 2), swap(total, "xy", 3)
    x_a = swap(message_a, "xy", 1)
    x_b = pairs(message_b, "xy")
    total = total + x_a[FACE:] + from_level(two + three, 1)
    half = lambda *dims: jax.ShapeDtypeStruct(dims, BF16)
    matrices = pl.pallas_call(
        prep_kernel,
        out_shape=(half(NZ + 8, LZ),) * 2
        + (half(NZ, LZ),) * 2
        + (half(LXY, PTS * NY),) * 2
        + (half(NP * NY, LXY),) * 2
        + (shape(EX, LXY, LZ),),
        in_specs=[VMEM] * 3,
        out_specs=(VMEM,) * 9,
        compiler_params=PARAMS,
        cost_estimate=cost(1_000_000_000, 1_000_000),
        name="prep",
    )(values, vectors, scale)

    def local(other, face):
        return pl.pallas_call(
            functools.partial(local_kernel, other),
            out_shape=shape(NP, NY, NZ),
            in_specs=[VMEM] * 13,
            out_specs=VMEM,
            compiler_params=PARAMS,
            cost_estimate=cost(1_000_000_000, 1_000_000),
            name="local",
        )(points, z_a, z_b, face, *matrices)

    total, matrices = lax.optimization_barrier((total, matrices))
    near = local(False, x_a)
    total = total + from_level(swap(total, "xy", 6), 2)
    total, near = lax.optimization_barrier((total, near))
    far = local(True, x_b)
    one, two, three = (swap(total, "xy", bits) for bits in (8, 16, 24))
    total = total + from_level(one, 3) + from_level(two + three, 4)
    total, far = lax.optimization_barrier((total, far))
    last = total[LAST:]
    last = last + (swap(last, "gz", 3) + swap(last, "gz", 5) + swap(last, "gz", 7))

    base = pl.pallas_call(
        middle_kernel,
        out_shape=shape(VERTS, 128),
        in_specs=[VMEM] * 4,
        out_specs=VMEM,
        compiler_params=PARAMS,
        cost_estimate=cost(7 * 512 * 512 * 2, 7_000_000),
        name="middle",
    )(aux, total, leaf_columns, separators)

    out, sol = pl.pallas_call(
        final_kernel,
        out_shape=(shape(NX, NY, NZ), shape(1, VERTS)),
        in_specs=[VMEM] * 6,
        out_specs=(VMEM, VMEM),
        compiler_params=PARAMS,
        cost_estimate=cost(512 * 512 * 2, 1_500_000),
        name="final",
    )(aux, last, base, near, far, separators)
    return out, sol.reshape(VERTS)


def solution(mesh):
    placed = (
        P("xy", None, "gz"),
        P(),
        P(),
        P("xy", None, "gz"),
        P("xy", None, "gz"),
        P(("gz", "xy"), None),
        P(("gz", "xy"), None),
        P(("gz", "xy"), None),
    )
    return jax.shard_map(
        per_device,
        mesh=mesh,
        in_specs=placed,
        out_specs=(P("xy", None, "gz"), P(("gz", "xy"))),
        check_vma=False,
    )
```

```python
import functools

import jax
import jax.numpy as jnp
from jax import lax
from jax.experimental import pallas as pl
from jax.experimental.pallas import tpu as pltpu
from jax.sharding import PartitionSpec as P

NP = 8
LEVELS = 6
EX, EY, EZ = 2, 4, 16
VERTS = 512
SW = 512
ELEMS = EX * EY * EZ
NX, NY, NZ = EX * NP, EY * NP, EZ * NP
PTS = NP + 2
CHUNKS = 8
ROWS = VERTS // CHUNKS

F32 = jnp.float32
BF16 = jnp.bfloat16
HIGH = lax.Precision.HIGHEST
VMEM = pl.BlockSpec(memory_space=pltpu.VMEM)
SMEM = pl.BlockSpec(memory_space=pltpu.SMEM)
ANY = pl.BlockSpec(memory_space=pl.ANY)
FIRST_LIMIT = 40 * 2**20
PARAMS = pltpu.CompilerParams(vmem_limit_bytes=40 * 1024 * 1024)
NN = (((1,), (0,)), ((), ()))
NT = (((1,), (1,)), ((), ()))


def dot(a, b, dims=NN):
    return lax.dot_general(a, b, dims, precision=HIGH, preferred_element_type=F32)


def bdot(a, b, dims=NN):
    return lax.dot_general(a, b, dims, preferred_element_type=F32)


def split(a):
    hi = a.astype(BF16)
    return hi, (a - hi.astype(F32)).astype(BF16)


def dot3(a, b, dims=NN):
    return bdot(a[0], b[0], dims) + (bdot(a[0], b[1], dims) + bdot(a[1], b[0], dims))


def iota(shape, axis):
    return lax.broadcasted_iota(jnp.int32, shape, axis)


def div_mod(values, by):
    quotient = jnp.floor((values.astype(F32) + 0.5) * (1.0 / by)).astype(jnp.int32)
    return quotient, values - quotient * by


def mark(condition):
    return condition.astype(F32)


def split3(a):
    hi = a.astype(BF16).astype(F32)
    rest = a - hi
    mid = rest.astype(BF16).astype(F32)
    return hi, mid, rest - mid


def dot_onehot(a, onehot):
    parts = jnp.concatenate([*split3(a), jnp.zeros_like(a)], axis=0).astype(BF16)
    out = bdot(parts, onehot.astype(BF16))
    return out[0:8] + (out[8:16] + out[16:24])


def odd(axis):
    return lax.rem(lax.axis_index(axis), 2)


def inside(axis, value):
    at = lax.axis_index(axis)
    return jnp.where((at > 0) & (at < lax.axis_size(axis) - 1), value, 0.0)


def factor(level):
    group = 256 if level == LEVELS - 1 else 2 ** (level + 1)
    return float(group) ** (-0.25)


def vertex_values(vm_row, row):
    out = []
    for g in range(VERTS // 8):
        vertex = (iota((8, ELEMS), 0) + g * 8).astype(F32)
        out.append(jnp.sum(jnp.where(vertex == vm_row, row, 0.0), axis=1, keepdims=True))
    return out


TILES = SW // 128
FACE = NY + 8
PARTIALS = LEVELS * TILES
LAST = PARTIALS - TILES
SUMS = 2 * LAST + TILES


def first_kernel(
    r_hbm, vm_hbm, mask_hbm, q_hbm, vec_hbm, lam_hbm, scale_hbm,
    face_a_ref, face_b_ref, out_ref, aux_ref, r_ref, q_ref, vec_ref, lam_ref, scale_ref,
    v_ref, m_ref, b_ref, sem,
):
    moves = (
        (r_hbm, r_ref), (vm_hbm, v_ref), (mask_hbm, m_ref),
        (vec_hbm, vec_ref), (lam_hbm, lam_ref), (scale_hbm, scale_ref),
    )
    small = [
        pltpu.make_async_copy(src, dst, sem.at[CHUNKS + i]) for i, (src, dst) in enumerate(moves)
    ]
    for copy in small:
        copy.start()
    large = []
    for c in range(CHUNKS):
        rows = pl.ds(c * ROWS, ROWS)
        large.append(pltpu.make_async_copy(q_hbm.at[rows], q_ref.at[rows], sem.at[c]))
        large[-1].start()
    small[1].wait()
    vm = jnp.concatenate([v_ref[0], v_ref[1]], axis=0).astype(F32)
    mine = (iota((8, ELEMS), 1) >> 4) == iota((8, ELEMS), 0)
    spread = mark(iota((EZ, ELEMS), 0) == (iota((EZ, ELEMS), 1) & (EZ - 1)))
    vm_row = jnp.sum(jnp.where(mine, dot_onehot(vm, spread), 0.0), axis=0, keepdims=True)
    small[2].wait()
    scales = []
    for level in range(LEVELS):
        value = m_ref[0:1, level : level + 1].astype(F32) * factor(level)
        scales.append(jnp.broadcast_to(value, (1, 128)))
        aux_ref[level : level + 1, :] = scales[-1]
    aux_ref[LEVELS : LEVELS + 1, :] = vm_row
    small[0].wait()
    sums = []
    for a in range(EX):
        total = r_ref[a * NP]
        for i in range(1, NP):
            total = total + r_ref[a * NP + i]
        sums.append(jnp.sum(total.reshape(EY, NP, NZ), axis=1))
    sums = jnp.concatenate(sums, axis=0) * (1.0 / NP**3)
    gather = mark((iota((NZ, ELEMS), 0) >> 3) == (iota((NZ, ELEMS), 1) & (EZ - 1)))
    means = jnp.sum(jnp.where(mine, dot_onehot(sums, gather), 0.0), axis=0, keepdims=True)
    aux_ref[LEVELS + 1 : LEVELS + 2, :] = means
    for g, value in enumerate(vertex_values(vm_row, means)):
        b_ref[g * 8 : g * 8 + 8, :] = jnp.broadcast_to(value, (8, 128))
    flat = r_ref[...].reshape(NX * NY, NZ)
    row, lane = iota((8, NZ), 0), iota((8, NZ), 1)
    side = odd("gz")
    lane_a = (1 - side) * (NZ - 1)
    lane_b = side * (NZ - 1)
    pick = mark(((row == 0) & (lane == lane_a)) | ((row == 1) & (lane == lane_b)))
    faces = dot(pick, flat, NT)
    for k in range(4):
        face_a_ref[k : k + 1, :] = faces[0:1, k * 128 : (k + 1) * 128]
        face_b_ref[k : k + 1, :] = faces[1:2, k * 128 : (k + 1) * 128]
    acc = [jnp.zeros((8, 128), F32) for _ in range(PARTIALS)]
    for c in range(CHUNKS):
        large[c].wait()
        for g in range(ROWS // 8):
            at = c * ROWS + g * 8
            b = b_ref[at : at + 8, :]
            for t in range(PARTIALS):
                acc[t] = acc[t] + q_ref[at : at + 8, t * 128 : (t + 1) * 128] * b
    for t in range(PARTIALS):
        total = jnp.sum(acc[t], axis=0, keepdims=True) * scales[t // TILES]
        out_ref[t : t + 1, :] = total
        face_a_ref[8 + t : 9 + t, :] = total
    for copy in small[3:]:
        copy.wait()


def join_kernel(partial_ref, za_ref, out_ref):
    side = odd("gz") == 1
    mine, other = partial_ref[...], za_ref[8 : 8 + PARTIALS, :]
    out_ref[0:LAST, :] = jnp.where(side, other, mine)[0:LAST]
    out_ref[LAST : 2 * LAST, :] = jnp.where(side, mine, other)[0:LAST]
    out_ref[2 * LAST : SUMS, :] = (mine + other)[LAST:]


def edge_kernel(r_ref, za_ref, zb_ref, sums_ref, a_ref, b_ref):
    side = odd("gz")
    za, zb = za_ref[0:4, :], inside("gz", zb_ref[...])
    low = jnp.where(side == 1, za, zb)
    high = jnp.where(side == 1, zb, za)
    turned = odd("xy") == 1
    first, last = r_ref[0], r_ref[NX - 1]
    for out, take in ((a_ref, turned), (b_ref, jnp.logical_not(turned))):
        out[0:NY, :] = jnp.where(take, first, last)
        out[NY:FACE, :] = jnp.zeros((8, NZ), F32)
        for i, edge in enumerate((low, high)):
            out[NY + i : NY + i + 1, 0:NY] = jnp.where(take, edge[0:1, 0:NY], edge[3:4, 128 - NY :])
    a_ref[FACE : FACE + SUMS, :] = sums_ref[...]


def middle_kernel(
    scale_ref, alpha_ref, leaf_ref, q_ref, near_ref, far_ref, in0_ref, in1_ref, out_ref, local_ref
):
    before = odd("xy") == 1
    near, far = near_ref[...], far_ref[...]
    bz_in = (in0_ref[...], in1_ref[...])
    for a, inner in enumerate((jnp.where(before, near, far), jnp.where(before, far, near))):
        result = dot3(split(inner), bz_in, NT)
        local_ref[a * NP : (a + 1) * NP] = result.reshape(NP, NY, NZ)
    acc = [jnp.zeros((8, 128), F32) for _ in range(TILES)]
    values = vertex_values(scale_ref[LEVELS : LEVELS + 1, :], scale_ref[LEVELS + 1 : LEVELS + 2, :])
    for g, b in enumerate(values):
        for t in range(TILES):
            acc[t] = acc[t] + leaf_ref[g * 8 : g * 8 + 8, t * 128 : (t + 1) * 128] * b
    leaf_alpha = [jnp.sum(acc[t], axis=0, keepdims=True) for t in range(TILES)]
    alpha = []
    side = odd("gz") == 1
    for t in range((LEVELS - 1) * TILES):
        level = t // TILES
        row = jnp.where(side, alpha_ref[LAST + t : LAST + t + 1, :], alpha_ref[t : t + 1, :])
        alpha.append(row * scale_ref[level : level + 1, :])
    for c in range(CHUNKS):
        rows = slice(c * ROWS, (c + 1) * ROWS)
        total = leaf_ref[rows, 0:128] * leaf_alpha[0]
        for t in range(1, TILES):
            total = total + leaf_ref[rows, t * 128 : (t + 1) * 128] * leaf_alpha[t]
        for t in range(len(alpha)):
            total = total + q_ref[rows, t * 128 : (t + 1) * 128] * alpha[t]
        out_ref[rows, :] = total


def final_kernel(scale_ref, alpha_ref, base_ref, local_ref, q_ref, out_ref, sol_ref):
    alpha = alpha_ref[...] * scale_ref[LEVELS - 1 : LEVELS, :]
    start = (LEVELS - 1) * SW
    vm_row = scale_ref[LEVELS : LEVELS + 1, :]
    acc = jnp.zeros((8, ELEMS), F32)
    totals = []
    for g in range(VERTS // 8):
        rows = slice(g * 8, g * 8 + 8)
        total = base_ref[rows, :]
        for t in range(TILES):
            at = start + t * 128
            total = total + q_ref[rows, at : at + 128] * alpha[t : t + 1, :]
        totals.append(total)
        value = jnp.sum(total, axis=1, keepdims=True)
        vertex = (iota((8, ELEMS), 0) + g * 8).astype(F32)
        acc = acc + jnp.where(vertex == vm_row, value, 0.0)
    per_element = jnp.sum(acc, axis=0, keepdims=True)
    mine = (iota((8, ELEMS), 1) >> 4) == iota((8, ELEMS), 0)
    spread = mark((iota((ELEMS, NZ), 0) & (EZ - 1)) == (iota((ELEMS, NZ), 1) >> 3))
    rows = dot_onehot(jnp.where(mine, per_element, 0.0), spread)
    for a in range(EX):
        add = jnp.broadcast_to(rows[a * EY : (a + 1) * EY, None, :], (EY, NP, NZ)).reshape(NY, NZ)
        for i in range(NP):
            out_ref[a * NP + i] = local_ref[a * NP + i] + add
    ones = jnp.ones((8, 128), BF16)
    row = [bdot(ones, part.astype(BF16), NT) for part in split3(jnp.concatenate(totals, axis=0))]
    sol_ref[...] = (row[0] + (row[1] + row[2]))[0:1]


LZ = EZ * PTS
LXY = PTS * EY * PTS


def prep_kernel(
    lam_ref, vec_ref, scale_ref, bz0_ref, bz1_ref, in0_ref, in1_ref, f0_ref, f1_ref, k0_ref, k1_ref, inv_ref
):
    lane = iota((NZ + 8, LZ), 1)
    z = iota((NZ + 8, LZ), 0)
    c, p = div_mod(lane, PTS)
    z = jnp.where(z < NZ, z, jnp.where(z == NZ, -1, jnp.where(z == NZ + 1, NZ, -1000)))
    place = z - NP * c + 1
    _, p10 = div_mod(iota((PTS, LZ), 1), PTS)
    repeat = mark(p10 == iota((PTS, LZ), 0))
    v2 = dot(vec_ref[:, 2, :], repeat)
    bz = jnp.zeros((NZ + 8, LZ), F32)
    for k in range(PTS):
        bz = jnp.where(place == k, v2[k : k + 1, :], bz)
    bz_in = jnp.where((place >= 1) & (place <= NP), bz, 0.0)[0:NZ]
    bz0_ref[...], bz1_ref[...] = split(bz)
    in0_ref[...], in1_ref[...] = split(bz_in)

    _, n = div_mod(iota((PTS, LXY), 1), PTS)
    m, _ = div_mod(iota((PTS, LXY), 1), PTS * EY)
    at = iota((PTS, LXY), 0)
    v1 = dot(vec_ref[:, 1, :], mark(n == at))
    v0 = dot(vec_ref[:, 0, :], mark(m == at))
    mb, _ = div_mod(iota((NY, LXY), 1), PTS)
    b = mb & (EY - 1)
    y = iota((NY, LXY), 0)
    place = y - NP * b + 1
    by = jnp.zeros((NY, LXY), F32)
    for j in range(PTS):
        by = jnp.where(place == j, v1[j : j + 1, :], by)
    by_in = jnp.where((place >= 1) & (place <= NP), by, 0.0)
    forward = jnp.concatenate([by * v0[i : i + 1, :] for i in range(PTS)], axis=0)
    f0_ref[...], f1_ref[...] = split(forward.T)
    back = jnp.concatenate([by_in * v0[i : i + 1, :] for i in range(1, NP + 1)], axis=0)
    k0_ref[...], k1_ref[...] = split(back)

    rows40 = EY * PTS
    rb, _ = div_mod(iota((rows40, EY), 0), PTS)
    pick_b = mark(rb == iota((rows40, EY), 1))
    lc, _ = div_mod(iota((EZ, LZ), 1), PTS)
    pick_c = mark(lc == iota((EZ, LZ), 0))
    _, rn = div_mod(iota((rows40, LZ), 0), PTS)
    _, lp = div_mod(iota((rows40, LZ), 1), PTS)
    lam = jnp.zeros((rows40, LZ), F32)
    lam2 = jnp.zeros((rows40, LZ), F32)
    for k in range(PTS):
        lam = jnp.where(rn == k, lam_ref[1:2, k : k + 1], lam)
        lam2 = jnp.where(lp == k, lam_ref[2:3, k : k + 1], lam2)
    for a in range(EX):
        factors = dot(dot(pick_b, scale_ref[a]), pick_c)
        for i in range(PTS):
            inv_ref[a, i * rows40 : (i + 1) * rows40, :] = 1.0 / (
                factors * ((lam_ref[0:1, i : i + 1] + lam) + lam2)
            )


def local_kernel(
    other, r_ref, za_ref, zb_ref, face_ref,
    bz0_ref, bz1_ref, f0_ref, f1_ref, k0_ref, k1_ref, inv_ref, out_ref,
):
    row = iota((8, 128), 0)
    side = odd("gz")
    za, zb = za_ref[0:4, :], inside("gz", zb_ref[...])
    zlow, zhigh = jnp.where(side == 1, za, zb), jnp.where(side == 1, zb, za)
    face = face_ref[0:FACE, :]
    if other:
        face = inside("xy", face)
    at = odd("xy") if other else 1 - odd("xy")
    before = at == 0
    sides = [
        jnp.where(row == 0, zlow[k : k + 1], jnp.where(row == 1, zhigh[k : k + 1], 0.0)).T
        for k in range(4)
    ]
    edge = face[NY:FACE].T[0:NY]
    own = r_ref[pl.ds(at * (NP - 1), NP + 1)].reshape((NP + 1) * NY, NZ)
    sides = jnp.concatenate(sides, axis=0)
    sides = jnp.where(before, sides[: (NP + 1) * NY], sides[(NP - 1) * NY :])
    points = jnp.where(
        before,
        jnp.concatenate([face[0:NY], own], axis=0),
        jnp.concatenate([own, face[0:NY]], axis=0),
    )
    sides = jnp.where(
        before, jnp.concatenate([edge, sides], axis=0), jnp.concatenate([sides, edge], axis=0)
    )
    points = jnp.concatenate([points, sides], axis=1)
    window = split(dot3(split(points), (bz0_ref[...], bz1_ref[...])))
    scaled = dot3((f0_ref[...], f1_ref[...]), window) * inv_ref[at]
    out_ref[...] = dot3((k0_ref[...], k1_ref[...]), split(scaled))


def shape(*dims):
    return jax.ShapeDtypeStruct(dims, F32)


def cost(flops, size):
    return pl.CostEstimate(flops=flops, bytes_accessed=size, transcendentals=0)


def per_device(
    residual,
    eigen_vectors,
    eigen_values,
    element_scale,
    vertex_map,
    leaf_columns,
    separator_columns,
    separator_mask,
):
    face_a, face_b, partial, aux, points, separators, vectors, values, scale = pl.pallas_call(
        first_kernel,
        out_shape=(
            shape(8 + PARTIALS, 128), shape(4, 128), shape(PARTIALS, 128), shape(8, 128),
            shape(NX, NY, NZ), shape(VERTS, LEVELS * SW),
            shape(PTS, 3, PTS), shape(3, PTS), shape(EX, EY, EZ),
        ),
        in_specs=[pl.BlockSpec(memory_space=pltpu.HBM)] * 7,
        out_specs=(VMEM,) * 9,
        scratch_shapes=[
            pltpu.VMEM((EX, EY, EZ), jnp.int32),
            pltpu.VMEM((1, LEVELS), jnp.int32),
            pltpu.VMEM((VERTS, 128), F32),
            pltpu.SemaphoreType.DMA((CHUNKS + 6,)),
        ],
        compiler_params=pltpu.CompilerParams(vmem_limit_bytes=FIRST_LIMIT),
        cost_estimate=cost(6 * 512 * 512 * 2, 6_500_000),
        name="first",
    )(
        *(
            pltpu.with_memory_space_constraint(x, pltpu.HBM)
            for x in (
                residual, vertex_map, separator_mask, separator_columns,
                eigen_vectors.transpose(1, 0, 2), eigen_values, element_scale,
            )
        )
    )

    def swap(value, axis, bits):
        return lax.ppermute(value, axis, [(i, i ^ bits) for i in range(lax.axis_size(axis))])

    def pairs(value, axis):
        count = lax.axis_size(axis)
        return lax.ppermute(value, axis, [(i, (i + 2 * (i % 2) - 1) % count) for i in range(count)])

    z_a = swap(face_a, "gz", 1)
    z_b = pairs(face_b, "gz")

    total = pl.pallas_call(
        join_kernel,
        out_shape=shape(SUMS, 128),
        in_specs=[VMEM] * 2,
        out_specs=VMEM,
        compiler_params=PARAMS,
        cost_estimate=cost(1000, 50_000),
        name="join",
    )(partial, z_a)

    message_a, message_b = pl.pallas_call(
        edge_kernel,
        out_shape=(shape(FACE + SUMS, NZ), shape(FACE, NZ)),
        in_specs=[VMEM] * 4,
        out_specs=(VMEM, VMEM),
        compiler_params=PARAMS,
        cost_estimate=cost(1000, 100_000),
        name="edges",
    )(points, z_a, z_b, total)

    row = jnp.arange(SUMS, dtype=jnp.int32)[:, None]
    level = jnp.where(row < 2 * LAST, row % LAST, LAST) // TILES

    def from_level(value, first):
        return jnp.where(level >= first, value, 0.0)

    def cross(value, bits):
        count = lax.axis_size("gz") * lax.axis_size("xy")
        partner = lax.axis_size("xy") ^ bits
        return lax.ppermute(value, ("gz", "xy"), [(i, i ^ partner) for i in range(count)])

    two, three = cross(total, 2), cross(total, 3)
    x_a = swap(message_a, "xy", 1)
    total = total + x_a[FACE:] + from_level(two + three, 1)
    half = lambda *dims: jax.ShapeDtypeStruct(dims, BF16)
    matrices = pl.pallas_call(
        prep_kernel,
        out_shape=(half(NZ + 8, LZ),) * 2
        + (half(NZ, LZ),) * 2
        + (half(LXY, PTS * NY),) * 2
        + (half(NP * NY, LXY),) * 2
        + (shape(EX, LXY, LZ),),
        in_specs=[VMEM] * 3,
        out_specs=(VMEM,) * 9,
        compiler_params=PARAMS,
        cost_estimate=cost(1_000_000_000, 1_000_000),
        name="prep",
    )(values, vectors, scale)

    def local(other, face):
        return pl.pallas_call(
            functools.partial(local_kernel, other),
            out_shape=shape(NP * NY, LZ),
            in_specs=[VMEM] * 11,
            out_specs=VMEM,
            compiler_params=PARAMS,
            cost_estimate=cost(1_000_000_000, 1_000_000),
            name="local",
        )(points, z_a, z_b, face, *matrices[:2], *matrices[4:])

    total, matrices, message_b = lax.optimization_barrier((total, matrices, message_b))
    x_b = pairs(message_b, "xy")
    near = local(False, x_a)
    total = total + from_level(cross(total, 6), 2)
    total, near = lax.optimization_barrier((total, near))
    far = local(True, x_b)
    one, two, three = (cross(total, bits) for bits in (8, 16, 24))
    total = total + from_level(one, 3) + from_level(two + three, 4)
    total, far = lax.optimization_barrier((total, far))
    last = total[2 * LAST :]
    last = last + (swap(last, "gz", 7) + swap(last, "gz", 3) + swap(last, "gz", 5))

    base, local = pl.pallas_call(
        middle_kernel,
        out_shape=(shape(VERTS, 128), shape(NX, NY, NZ)),
        in_specs=[VMEM] * 8,
        out_specs=(VMEM, VMEM),
        compiler_params=PARAMS,
        cost_estimate=cost(7 * 512 * 512 * 2, 7_000_000),
        name="middle",
    )(aux, total, leaf_columns, separators, near, far, matrices[2], matrices[3])

    out, sol = pl.pallas_call(
        final_kernel,
        out_shape=(shape(NX, NY, NZ), shape(1, VERTS)),
        in_specs=[VMEM] * 5,
        out_specs=(VMEM, VMEM),
        compiler_params=PARAMS,
        cost_estimate=cost(512 * 512 * 2, 1_500_000),
        name="final",
    )(aux, last, base, local, separators)
    return out, sol.reshape(VERTS)


def solution(mesh):
    placed = (
        P("xy", None, "gz"),
        P(),
        P(),
        P("xy", None, "gz"),
        P("xy", None, "gz"),
        P(("gz", "xy"), None),
        P(("gz", "xy"), None),
        P(("gz", "xy"), None),
    )
    return jax.shard_map(
        per_device,
        mesh=mesh,
        in_specs=placed,
        out_specs=(P("xy", None, "gz"), P(("gz", "xy"))),
        check_vma=False,
    )
```

```python
import functools

import jax
import jax.numpy as jnp
from jax import lax
from jax.experimental import pallas as pl
from jax.experimental.pallas import tpu as pltpu
from jax.sharding import PartitionSpec as P

NP = 8
LEVELS = 6
EX, EY, EZ = 2, 4, 16
VERTS = 512
SW = 512
ELEMS = EX * EY * EZ
NX, NY, NZ = EX * NP, EY * NP, EZ * NP
PTS = NP + 2
CHUNKS = 8
ROWS = VERTS // CHUNKS

F32 = jnp.float32
BF16 = jnp.bfloat16
HIGH = lax.Precision.HIGHEST
VMEM = pl.BlockSpec(memory_space=pltpu.VMEM)
FIRST_LIMIT = 40 * 2**20
PARAMS = pltpu.CompilerParams(vmem_limit_bytes=40 * 1024 * 1024)
NN = (((1,), (0,)), ((), ()))
NT = (((1,), (1,)), ((), ()))


def dot(a, b, dims=NN):
    return lax.dot_general(a, b, dims, precision=HIGH, preferred_element_type=F32)


def bdot(a, b, dims=NN):
    return lax.dot_general(a, b, dims, preferred_element_type=F32)


def split(a):
    hi = a.astype(BF16)
    return hi, (a - hi.astype(F32)).astype(BF16)


def dot3(a, b, dims=NN):
    return bdot(a[0], b[0], dims) + (bdot(a[0], b[1], dims) + bdot(a[1], b[0], dims))


def iota(shape, axis):
    return lax.broadcasted_iota(jnp.int32, shape, axis)


def div_mod(values, by):
    quotient = jnp.floor((values.astype(F32) + 0.5) * (1.0 / by)).astype(jnp.int32)
    return quotient, values - quotient * by


def mark(condition):
    return condition.astype(F32)


def split3(a):
    hi = a.astype(BF16).astype(F32)
    rest = a - hi
    mid = rest.astype(BF16).astype(F32)
    return hi, mid, rest - mid


def dot_onehot(a, onehot):
    parts = jnp.concatenate([*split3(a), jnp.zeros_like(a)], axis=0).astype(BF16)
    out = bdot(parts, onehot.astype(BF16))
    return out[0:8] + (out[8:16] + out[16:24])


def odd(axis):
    return lax.rem(lax.axis_index(axis), 2)


def inside(axis, value):
    at = lax.axis_index(axis)
    return jnp.where((at > 0) & (at < lax.axis_size(axis) - 1), value, 0.0)


def factor(level):
    group = 256 if level == LEVELS - 1 else 2 ** (level + 1)
    return float(group) ** (-0.25)


def vertex_values(vm_row, row):
    out = []
    for g in range(VERTS // 8):
        vertex = (iota((8, ELEMS), 0) + g * 8).astype(F32)
        out.append(jnp.sum(jnp.where(vertex == vm_row, row, 0.0), axis=1, keepdims=True))
    return out


TILES = SW // 128
FACE = NY + 8
PARTIALS = LEVELS * TILES
LAST = PARTIALS - TILES
SUMS = 2 * LAST + TILES


def first_kernel(
    r_hbm, vm_hbm, mask_hbm, q_hbm, vec_hbm, lam_hbm, scale_hbm,
    face_a_ref, face_b_ref, out_ref, aux_ref, r_ref, q_ref, vec_ref, lam_ref, scale_ref,
    v_ref, m_ref, b_ref, sem,
):
    moves = (
        (r_hbm, r_ref), (vm_hbm, v_ref), (mask_hbm, m_ref),
        (vec_hbm, vec_ref), (lam_hbm, lam_ref), (scale_hbm, scale_ref),
    )
    small = [
        pltpu.make_async_copy(src, dst, sem.at[CHUNKS + i]) for i, (src, dst) in enumerate(moves)
    ]
    for copy in small:
        copy.start()
    large = []
    for c in range(CHUNKS):
        rows = pl.ds(c * ROWS, ROWS)
        large.append(pltpu.make_async_copy(q_hbm.at[rows], q_ref.at[rows], sem.at[c]))
        large[-1].start()
    small[1].wait()
    vm = jnp.concatenate([v_ref[0], v_ref[1]], axis=0).astype(F32)
    mine = (iota((8, ELEMS), 1) >> 4) == iota((8, ELEMS), 0)
    spread = mark(iota((EZ, ELEMS), 0) == (iota((EZ, ELEMS), 1) & (EZ - 1)))
    vm_row = jnp.sum(jnp.where(mine, dot_onehot(vm, spread), 0.0), axis=0, keepdims=True)
    small[2].wait()
    scales = []
    for level in range(LEVELS):
        value = m_ref[0:1, level : level + 1].astype(F32) * factor(level)
        scales.append(jnp.broadcast_to(value, (1, 128)))
        aux_ref[level : level + 1, :] = scales[-1]
    aux_ref[LEVELS : LEVELS + 1, :] = vm_row
    small[0].wait()
    sums = []
    for a in range(EX):
        total = r_ref[a * NP]
        for i in range(1, NP):
            total = total + r_ref[a * NP + i]
        sums.append(jnp.sum(total.reshape(EY, NP, NZ), axis=1))
    sums = jnp.concatenate(sums, axis=0) * (1.0 / NP**3)
    gather = mark((iota((NZ, ELEMS), 0) >> 3) == (iota((NZ, ELEMS), 1) & (EZ - 1)))
    means = jnp.sum(jnp.where(mine, dot_onehot(sums, gather), 0.0), axis=0, keepdims=True)
    aux_ref[LEVELS + 1 : LEVELS + 2, :] = means
    for g, value in enumerate(vertex_values(vm_row, means)):
        b_ref[g * 8 : g * 8 + 8, :] = jnp.broadcast_to(value, (8, 128))
    flat = r_ref[...].reshape(NX * NY, NZ)
    row, lane = iota((8, NZ), 0), iota((8, NZ), 1)
    side = odd("gz")
    lane_a = (1 - side) * (NZ - 1)
    lane_b = side * (NZ - 1)
    pick = mark(((row == 0) & (lane == lane_a)) | ((row == 1) & (lane == lane_b)))
    faces = dot(pick, flat, NT)
    for k in range(4):
        face_a_ref[k : k + 1, :] = faces[0:1, k * 128 : (k + 1) * 128]
        face_b_ref[k : k + 1, :] = faces[1:2, k * 128 : (k + 1) * 128]
    acc = [jnp.zeros((8, 128), F32) for _ in range(PARTIALS)]
    for c in range(CHUNKS):
        large[c].wait()
        for g in range(ROWS // 8):
            at = c * ROWS + g * 8
            b = b_ref[at : at + 8, :]
            for t in range(PARTIALS):
                acc[t] = acc[t] + q_ref[at : at + 8, t * 128 : (t + 1) * 128] * b
    for t in range(PARTIALS):
        total = jnp.sum(acc[t], axis=0, keepdims=True) * scales[t // TILES]
        out_ref[t : t + 1, :] = total
        face_a_ref[8 + t : 9 + t, :] = total
    for copy in small[3:]:
        copy.wait()


def join_kernel(partial_ref, za_ref, out_ref):
    side = odd("gz") == 1
    mine, other = partial_ref[...], za_ref[8 : 8 + PARTIALS, :]
    out_ref[0:LAST, :] = jnp.where(side, other, mine)[0:LAST]
    out_ref[LAST : 2 * LAST, :] = jnp.where(side, mine, other)[0:LAST]
    out_ref[2 * LAST : SUMS, :] = (mine + other)[LAST:]


def edge_kernel(r_ref, za_ref, zb_ref, sums_ref, a_ref, b_ref):
    side = odd("gz")
    za, zb = za_ref[0:4, :], inside("gz", zb_ref[...])
    low = jnp.where(side == 1, za, zb)
    high = jnp.where(side == 1, zb, za)
    turned = odd("xy") == 1
    first, last = r_ref[0], r_ref[NX - 1]
    for out, take in ((a_ref, turned), (b_ref, jnp.logical_not(turned))):
        out[0:NY, :] = jnp.where(take, first, last)
        out[NY:FACE, :] = jnp.zeros((8, NZ), F32)
        for i, edge in enumerate((low, high)):
            out[NY + i : NY + i + 1, 0:NY] = jnp.where(take, edge[0:1, 0:NY], edge[3:4, 128 - NY :])
    a_ref[FACE : FACE + SUMS, :] = sums_ref[...]


def middle_kernel(
    scale_ref, alpha_ref, leaf_ref, q_ref, near_ref, far_ref, in0_ref, in1_ref, out_ref, local_ref
):
    before = odd("xy") == 1
    near, far = near_ref[...], far_ref[...]
    bz_in = (in0_ref[...], in1_ref[...])
    for a, inner in enumerate((jnp.where(before, near, far), jnp.where(before, far, near))):
        result = dot3(split(inner), bz_in, NT)
        local_ref[a * NP : (a + 1) * NP] = result.reshape(NP, NY, NZ)
    acc = [jnp.zeros((8, 128), F32) for _ in range(TILES)]
    values = vertex_values(scale_ref[LEVELS : LEVELS + 1, :], scale_ref[LEVELS + 1 : LEVELS + 2, :])
    for g, b in enumerate(values):
        for t in range(TILES):
            acc[t] = acc[t] + leaf_ref[g * 8 : g * 8 + 8, t * 128 : (t + 1) * 128] * b
    leaf_alpha = [jnp.sum(acc[t], axis=0, keepdims=True) for t in range(TILES)]
    alpha = []
    side = odd("gz") == 1
    for t in range((LEVELS - 1) * TILES):
        level = t // TILES
        row = jnp.where(side, alpha_ref[LAST + t : LAST + t + 1, :], alpha_ref[t : t + 1, :])
        alpha.append(row * scale_ref[level : level + 1, :])
    for c in range(CHUNKS):
        rows = slice(c * ROWS, (c + 1) * ROWS)
        total = leaf_ref[rows, 0:128] * leaf_alpha[0]
        for t in range(1, TILES):
            total = total + leaf_ref[rows, t * 128 : (t + 1) * 128] * leaf_alpha[t]
        for t in range(len(alpha)):
            total = total + q_ref[rows, t * 128 : (t + 1) * 128] * alpha[t]
        out_ref[rows, :] = total


def final_kernel(scale_ref, alpha_ref, base_ref, local_ref, q_ref, out_ref, sol_ref):
    alpha = alpha_ref[...] * scale_ref[LEVELS - 1 : LEVELS, :]
    start = (LEVELS - 1) * SW
    vm_row = scale_ref[LEVELS : LEVELS + 1, :]
    acc = jnp.zeros((8, ELEMS), F32)
    turned = [jnp.zeros((8, 128), F32) for _ in range(VERTS // 128)]
    for g in range(VERTS // 8):
        rows = slice(g * 8, g * 8 + 8)
        total = base_ref[rows, :]
        for t in range(TILES):
            at = start + t * 128
            total = total + q_ref[rows, at : at + 128] * alpha[t : t + 1, :]
        value = jnp.sum(total, axis=1, keepdims=True)
        lane = iota((8, 128), 0) + (g % 16) * 8
        turned[g // 16] = turned[g // 16] + jnp.where(iota((8, 128), 1) == lane, value, 0.0)
        vertex = (iota((8, ELEMS), 0) + g * 8).astype(F32)
        acc = acc + jnp.where(vertex == vm_row, value, 0.0)
    per_element = jnp.sum(acc, axis=0, keepdims=True)
    mine = (iota((8, ELEMS), 1) >> 4) == iota((8, ELEMS), 0)
    spread = mark((iota((ELEMS, NZ), 0) & (EZ - 1)) == (iota((ELEMS, NZ), 1) >> 3))
    rows = dot_onehot(jnp.where(mine, per_element, 0.0), spread)
    for a in range(EX):
        add = jnp.broadcast_to(rows[a * EY : (a + 1) * EY, None, :], (EY, NP, NZ)).reshape(NY, NZ)
        for i in range(NP):
            out_ref[a * NP + i] = local_ref[a * NP + i] + add
    for k, rows in enumerate(turned):
        sol_ref[:, k * 128 : (k + 1) * 128] = jnp.sum(rows, axis=0, keepdims=True)


LZ = EZ * PTS
LXY = PTS * EY * PTS


def prep_kernel(
    lam_ref, vec_ref, scale_ref, r_ref, za_ref, zb_ref,
    bz0_ref, bz1_ref, in0_ref, in1_ref, f0_ref, f1_ref, k0_ref, k1_ref, inv_ref, s0_ref, s1_ref,
):
    lane = iota((NZ + 8, LZ), 1)
    z = iota((NZ + 8, LZ), 0)
    c, p = div_mod(lane, PTS)
    z = jnp.where(z < NZ, z, jnp.where(z == NZ, -1, jnp.where(z == NZ + 1, NZ, -1000)))
    place = z - NP * c + 1
    _, p10 = div_mod(iota((PTS, LZ), 1), PTS)
    repeat = mark(p10 == iota((PTS, LZ), 0))
    v2 = dot(vec_ref[:, 2, :], repeat)
    bz = jnp.zeros((NZ + 8, LZ), F32)
    for k in range(PTS):
        bz = jnp.where(place == k, v2[k : k + 1, :], bz)
    bz_in = jnp.where((place >= 1) & (place <= NP), bz, 0.0)[0:NZ]
    bz = split(bz)
    bz0_ref[...], bz1_ref[...] = bz
    in0_ref[...], in1_ref[...] = split(bz_in)

    row = iota((8, 128), 0)
    side = odd("gz")
    za, zb = za_ref[0:4, :], inside("gz", zb_ref[...])
    zlow, zhigh = jnp.where(side == 1, za, zb), jnp.where(side == 1, zb, za)
    sides = [
        jnp.where(row == 0, zlow[k : k + 1], jnp.where(row == 1, zhigh[k : k + 1], 0.0)).T
        for k in range(4)
    ]
    own = jnp.concatenate([r_ref[...].reshape(NX * NY, NZ), jnp.concatenate(sides, axis=0)], axis=1)
    s0_ref[...], s1_ref[...] = split(dot3(split(own), bz))

    _, n = div_mod(iota((PTS, LXY), 1), PTS)
    m, _ = div_mod(iota((PTS, LXY), 1), PTS * EY)
    at = iota((PTS, LXY), 0)
    v1 = dot(vec_ref[:, 1, :], mark(n == at))
    v0 = dot(vec_ref[:, 0, :], mark(m == at))
    mb, _ = div_mod(iota((NY, LXY), 1), PTS)
    b = mb & (EY - 1)
    y = iota((NY, LXY), 0)
    place = y - NP * b + 1
    by = jnp.zeros((NY, LXY), F32)
    for j in range(PTS):
        by = jnp.where(place == j, v1[j : j + 1, :], by)
    by_in = jnp.where((place >= 1) & (place <= NP), by, 0.0)
    forward = jnp.concatenate([by * v0[i : i + 1, :] for i in range(PTS)], axis=0)
    f0_ref[...], f1_ref[...] = split(forward.T)
    back = jnp.concatenate([by_in * v0[i : i + 1, :] for i in range(1, NP + 1)], axis=0)
    k0_ref[...], k1_ref[...] = split(back)

    rows40 = EY * PTS
    rb, _ = div_mod(iota((rows40, EY), 0), PTS)
    pick_b = mark(rb == iota((rows40, EY), 1))
    lc, _ = div_mod(iota((EZ, LZ), 1), PTS)
    pick_c = mark(lc == iota((EZ, LZ), 0))
    _, rn = div_mod(iota((rows40, LZ), 0), PTS)
    _, lp = div_mod(iota((rows40, LZ), 1), PTS)
    lam = jnp.zeros((rows40, LZ), F32)
    lam2 = jnp.zeros((rows40, LZ), F32)
    for k in range(PTS):
        lam = jnp.where(rn == k, lam_ref[1:2, k : k + 1], lam)
        lam2 = jnp.where(lp == k, lam_ref[2:3, k : k + 1], lam2)
    for a in range(EX):
        factors = dot(dot(pick_b, scale_ref[a]), pick_c)
        for i in range(PTS):
            inv_ref[a, i * rows40 : (i + 1) * rows40, :] = 1.0 / (
                factors * ((lam_ref[0:1, i : i + 1] + lam) + lam2)
            )


def local_kernel(
    other, s0_ref, s1_ref, face_ref,
    bz0_ref, bz1_ref, f0_ref, f1_ref, k0_ref, k1_ref, inv_ref, out_ref, w0_ref, w1_ref,
):
    face = face_ref[0:FACE, :]
    if other:
        face = inside("xy", face)
    at = odd("xy") if other else 1 - odd("xy")
    points = jnp.concatenate([face[0:NY], face[NY:FACE].T[0:NY]], axis=1)
    edge = split(dot3(split(points), (bz0_ref[...], bz1_ref[...])))
    size = (NP + 1) * NY
    own_from = pl.multiple_of(at * ((NP - 1) * NY), NY)
    own_to = pl.multiple_of((1 - at) * NY, NY)
    edge_to = pl.multiple_of(at * size, NY)
    for s_ref, w_ref, part in ((s0_ref, w0_ref, edge[0]), (s1_ref, w1_ref, edge[1])):
        w_ref[pl.ds(own_to, size), :] = s_ref[pl.ds(own_from, size), :]
        w_ref[pl.ds(edge_to, NY), :] = part
    scaled = dot3((f0_ref[...], f1_ref[...]), (w0_ref[...], w1_ref[...])) * inv_ref[at]
    out_ref[...] = dot3((k0_ref[...], k1_ref[...]), split(scaled))


def shape(*dims):
    return jax.ShapeDtypeStruct(dims, F32)


def cost(flops, size):
    return pl.CostEstimate(flops=flops, bytes_accessed=size, transcendentals=0)


def per_device(
    residual,
    eigen_vectors,
    eigen_values,
    element_scale,
    vertex_map,
    leaf_columns,
    separator_columns,
    separator_mask,
):
    face_a, face_b, partial, aux, points, separators, vectors, values, scale = pl.pallas_call(
        first_kernel,
        out_shape=(
            shape(8 + PARTIALS, 128), shape(4, 128), shape(PARTIALS, 128), shape(8, 128),
            shape(NX, NY, NZ), shape(VERTS, LEVELS * SW),
            shape(PTS, 3, PTS), shape(3, PTS), shape(EX, EY, EZ),
        ),
        in_specs=[pl.BlockSpec(memory_space=pltpu.HBM)] * 7,
        out_specs=(VMEM,) * 9,
        scratch_shapes=[
            pltpu.VMEM((EX, EY, EZ), jnp.int32),
            pltpu.VMEM((1, LEVELS), jnp.int32),
            pltpu.VMEM((VERTS, 128), F32),
            pltpu.SemaphoreType.DMA((CHUNKS + 6,)),
        ],
        compiler_params=pltpu.CompilerParams(vmem_limit_bytes=FIRST_LIMIT),
        cost_estimate=cost(6 * 512 * 512 * 2, 6_500_000),
        name="first",
    )(
        *(
            pltpu.with_memory_space_constraint(x, pltpu.HBM)
            for x in (
                residual, vertex_map, separator_mask, separator_columns,
                eigen_vectors.transpose(1, 0, 2), eigen_values, element_scale,
            )
        )
    )

    def swap(value, axis, bits):
        return lax.ppermute(value, axis, [(i, i ^ bits) for i in range(lax.axis_size(axis))])

    def pairs(value, axis):
        count = lax.axis_size(axis)
        return lax.ppermute(value, axis, [(i, (i + 2 * (i % 2) - 1) % count) for i in range(count)])

    z_a = swap(face_a, "gz", 1)
    z_b = pairs(face_b, "gz")

    total = pl.pallas_call(
        join_kernel,
        out_shape=shape(SUMS, 128),
        in_specs=[VMEM] * 2,
        out_specs=VMEM,
        compiler_params=PARAMS,
        cost_estimate=cost(1000, 50_000),
        name="join",
    )(partial, z_a)

    message_a, message_b = pl.pallas_call(
        edge_kernel,
        out_shape=(shape(FACE + SUMS, NZ), shape(FACE, NZ)),
        in_specs=[VMEM] * 4,
        out_specs=(VMEM, VMEM),
        compiler_params=PARAMS,
        cost_estimate=cost(1000, 100_000),
        name="edges",
    )(points, z_a, z_b, total)

    row = jnp.arange(SUMS, dtype=jnp.int32)[:, None]
    level = jnp.where(row < 2 * LAST, row % LAST, LAST) // TILES

    def from_level(value, first):
        return jnp.where(level >= first, value, 0.0)

    def cross(value, bits):
        count = lax.axis_size("gz") * lax.axis_size("xy")
        partner = lax.axis_size("xy") ^ bits
        return lax.ppermute(value, ("gz", "xy"), [(i, i ^ partner) for i in range(count)])

    two, three = cross(total, 2), cross(total, 3)
    x_a = swap(message_a, "xy", 1)
    total = total + x_a[FACE:] + from_level(two + three, 1)
    half = lambda *dims: jax.ShapeDtypeStruct(dims, BF16)
    matrices = pl.pallas_call(
        prep_kernel,
        out_shape=(half(NZ + 8, LZ),) * 2
        + (half(NZ, LZ),) * 2
        + (half(LXY, PTS * NY),) * 2
        + (half(NP * NY, LXY),) * 2
        + (shape(EX, LXY, LZ),)
        + (half(NX * NY, LZ),) * 2,
        in_specs=[VMEM] * 6,
        out_specs=(VMEM,) * 11,
        compiler_params=PARAMS,
        cost_estimate=cost(1_000_000_000, 1_000_000),
        name="prep",
    )(values, vectors, scale, points, z_a, z_b)

    def local(other, face):
        return pl.pallas_call(
            functools.partial(local_kernel, other),
            out_shape=shape(NP * NY, LZ),
            in_specs=[VMEM] * 10,
            out_specs=VMEM,
            scratch_shapes=[pltpu.VMEM((PTS * NY, LZ), BF16)] * 2,
            compiler_params=PARAMS,
            cost_estimate=cost(1_000_000_000, 1_000_000),
            name="local",
        )(*matrices[9:], face, *matrices[:2], *matrices[4:9])

    total, matrices, message_b = lax.optimization_barrier((total, matrices, message_b))
    x_b = pairs(message_b, "xy")
    near = local(False, x_a)
    total = total + from_level(cross(total, 6), 2)
    total, near = lax.optimization_barrier((total, near))
    far = local(True, x_b)
    one, two, three = (cross(total, bits) for bits in (8, 16, 24))
    total = total + from_level(one, 3) + from_level(two + three, 4)
    total, far = lax.optimization_barrier((total, far))
    last = total[2 * LAST :]
    last = last + (swap(last, "gz", 7) + swap(last, "gz", 3) + swap(last, "gz", 5))

    base, local = pl.pallas_call(
        middle_kernel,
        out_shape=(shape(VERTS, 128), shape(NX, NY, NZ)),
        in_specs=[VMEM] * 8,
        out_specs=(VMEM, VMEM),
        compiler_params=PARAMS,
        cost_estimate=cost(7 * 512 * 512 * 2, 7_000_000),
        name="middle",
    )(aux, total, leaf_columns, separators, near, far, matrices[2], matrices[3])

    out, sol = pl.pallas_call(
        final_kernel,
        out_shape=(shape(NX, NY, NZ), shape(1, VERTS)),
        in_specs=[VMEM] * 5,
        out_specs=(VMEM, VMEM),
        compiler_params=PARAMS,
        cost_estimate=cost(512 * 512 * 2, 1_500_000),
        name="final",
    )(aux, last, base, local, separators)
    return out, sol.reshape(VERTS)


def solution(mesh):
    placed = (
        P("xy", None, "gz"),
        P(),
        P(),
        P("xy", None, "gz"),
        P("xy", None, "gz"),
        P(("gz", "xy"), None),
        P(("gz", "xy"), None),
        P(("gz", "xy"), None),
    )
    return jax.shard_map(
        per_device,
        mesh=mesh,
        in_specs=placed,
        out_specs=(P("xy", None, "gz"), P(("gz", "xy"))),
        check_vma=False,
    )
```

```python
import functools

import jax
import jax.numpy as jnp
from jax import lax
from jax.experimental import pallas as pl
from jax.experimental.pallas import tpu as pltpu
from jax.sharding import PartitionSpec as P

NP = 8
LEVELS = 6
EX, EY, EZ = 2, 4, 16
VERTS = 512
SW = 512
ELEMS = EX * EY * EZ
NX, NY, NZ = EX * NP, EY * NP, EZ * NP
PTS = NP + 2
CHUNKS = 8
ROWS = VERTS // CHUNKS

F32 = jnp.float32
BF16 = jnp.bfloat16
HIGH = lax.Precision.HIGHEST
VMEM = pl.BlockSpec(memory_space=pltpu.VMEM)
FIRST_LIMIT = 40 * 2**20
PARAMS = pltpu.CompilerParams(vmem_limit_bytes=40 * 1024 * 1024)
NN = (((1,), (0,)), ((), ()))
NT = (((1,), (1,)), ((), ()))


def dot(a, b, dims=NN):
    return lax.dot_general(a, b, dims, precision=HIGH, preferred_element_type=F32)


def bdot(a, b, dims=NN):
    return lax.dot_general(a, b, dims, preferred_element_type=F32)


def split(a):
    hi = a.astype(BF16)
    return hi, (a - hi.astype(F32)).astype(BF16)


def dot3(a, b, dims=NN):
    return bdot(a[0], b[0], dims) + (bdot(a[0], b[1], dims) + bdot(a[1], b[0], dims))


def iota(shape, axis):
    return lax.broadcasted_iota(jnp.int32, shape, axis)


def div_mod(values, by):
    quotient = jnp.floor((values.astype(F32) + 0.5) * (1.0 / by)).astype(jnp.int32)
    return quotient, values - quotient * by


def mark(condition):
    return condition.astype(F32)


def split3(a):
    hi = a.astype(BF16).astype(F32)
    rest = a - hi
    mid = rest.astype(BF16).astype(F32)
    return hi, mid, rest - mid


def dot_onehot(a, onehot):
    parts = jnp.concatenate([*split3(a), jnp.zeros_like(a)], axis=0).astype(BF16)
    out = bdot(parts, onehot.astype(BF16))
    return out[0:8] + (out[8:16] + out[16:24])


def odd(axis):
    return lax.rem(lax.axis_index(axis), 2)


def inside(axis, value):
    at = lax.axis_index(axis)
    return jnp.where((at > 0) & (at < lax.axis_size(axis) - 1), value, 0.0)


def factor(level):
    group = 256 if level == LEVELS - 1 else 2 ** (level + 1)
    return float(group) ** (-0.25)


def vertex_values(vm_row, row):
    out = []
    for g in range(VERTS // 8):
        vertex = (iota((8, ELEMS), 0) + g * 8).astype(F32)
        out.append(jnp.sum(jnp.where(vertex == vm_row, row, 0.0), axis=1, keepdims=True))
    return out


TILES = SW // 128
FACE = NY + 8
PARTIALS = LEVELS * TILES
LAST = PARTIALS - TILES
SUMS = 2 * LAST + TILES


def first_kernel(
    r_hbm, vm_hbm, mask_hbm, q_hbm, vec_hbm, lam_hbm, scale_hbm,
    face_a_ref, face_b_ref, out_ref, aux_ref, r_ref, q_ref, vec_ref, lam_ref, scale_ref,
    v_ref, m_ref, b_ref, sem,
):
    moves = (
        (r_hbm, r_ref), (vm_hbm, v_ref), (mask_hbm, m_ref),
        (vec_hbm, vec_ref), (lam_hbm, lam_ref), (scale_hbm, scale_ref),
    )
    small = [
        pltpu.make_async_copy(src, dst, sem.at[CHUNKS + i]) for i, (src, dst) in enumerate(moves)
    ]
    for copy in small:
        copy.start()
    large = []
    for c in range(CHUNKS):
        rows = pl.ds(c * ROWS, ROWS)
        large.append(pltpu.make_async_copy(q_hbm.at[rows], q_ref.at[rows], sem.at[c]))
        large[-1].start()
    small[1].wait()
    vm = jnp.concatenate([v_ref[0], v_ref[1]], axis=0).astype(F32)
    mine = (iota((8, ELEMS), 1) >> 4) == iota((8, ELEMS), 0)
    spread = mark(iota((EZ, ELEMS), 0) == (iota((EZ, ELEMS), 1) & (EZ - 1)))
    vm_row = jnp.sum(jnp.where(mine, dot_onehot(vm, spread), 0.0), axis=0, keepdims=True)
    small[2].wait()
    scales = []
    for level in range(LEVELS):
        value = m_ref[0:1, level : level + 1].astype(F32) * factor(level)
        scales.append(jnp.broadcast_to(value, (1, 128)))
        aux_ref[level : level + 1, :] = scales[-1]
    aux_ref[LEVELS : LEVELS + 1, :] = vm_row
    small[0].wait()
    sums = []
    for a in range(EX):
        total = r_ref[a * NP]
        for i in range(1, NP):
            total = total + r_ref[a * NP + i]
        sums.append(jnp.sum(total.reshape(EY, NP, NZ), axis=1))
    sums = jnp.concatenate(sums, axis=0) * (1.0 / NP**3)
    gather = mark((iota((NZ, ELEMS), 0) >> 3) == (iota((NZ, ELEMS), 1) & (EZ - 1)))
    means = jnp.sum(jnp.where(mine, dot_onehot(sums, gather), 0.0), axis=0, keepdims=True)
    aux_ref[LEVELS + 1 : LEVELS + 2, :] = means
    for g, value in enumerate(vertex_values(vm_row, means)):
        b_ref[g * 8 : g * 8 + 8, :] = jnp.broadcast_to(value, (8, 128))
    flat = r_ref[...].reshape(NX * NY, NZ)
    row, lane = iota((8, NZ), 0), iota((8, NZ), 1)
    side = odd("gz")
    lane_a = (1 - side) * (NZ - 1)
    lane_b = side * (NZ - 1)
    pick = mark(((row == 0) & (lane == lane_a)) | ((row == 1) & (lane == lane_b)))
    faces = dot(pick, flat, NT)
    for k in range(4):
        face_a_ref[k : k + 1, :] = faces[0:1, k * 128 : (k + 1) * 128]
        face_b_ref[k : k + 1, :] = faces[1:2, k * 128 : (k + 1) * 128]
    acc = [jnp.zeros((8, 128), F32) for _ in range(PARTIALS)]
    for c in range(CHUNKS):
        large[c].wait()
        for g in range(ROWS // 8):
            at = c * ROWS + g * 8
            b = b_ref[at : at + 8, :]
            for t in range(PARTIALS):
                acc[t] = acc[t] + q_ref[at : at + 8, t * 128 : (t + 1) * 128] * b
    for t in range(PARTIALS):
        total = jnp.sum(acc[t], axis=0, keepdims=True) * scales[t // TILES]
        out_ref[t : t + 1, :] = total
        face_a_ref[8 + t : 9 + t, :] = total
    for copy in small[3:]:
        copy.wait()


def sums_row(level, core):
    return TILES + (LEVELS - 2 - level) * 2 * TILES + core * TILES


def sums_from(level):
    return TILES + (LEVELS - 1 - level) * 2 * TILES


def join_kernel(partial_ref, za_ref, out_ref):
    side = odd("gz") == 1
    mine, other = partial_ref[...], za_ref[8 : 8 + PARTIALS, :]
    out_ref[0:TILES, :] = (mine + other)[LAST:]
    for core, rows in enumerate((jnp.where(side, other, mine), jnp.where(side, mine, other))):
        for level in range(LEVELS - 1):
            at = sums_row(level, core)
            out_ref[at : at + TILES, :] = rows[level * TILES : (level + 1) * TILES]


def edge_kernel(r_ref, za_ref, zb_ref, sums_ref, a_ref, b_ref):
    side = odd("gz")
    za, zb = za_ref[0:4, :], inside("gz", zb_ref[...])
    low = jnp.where(side == 1, za, zb)
    high = jnp.where(side == 1, zb, za)
    turned = odd("xy") == 1
    first, last = r_ref[0], r_ref[NX - 1]
    for out, take in ((a_ref, turned), (b_ref, jnp.logical_not(turned))):
        out[0:NY, :] = jnp.where(take, first, last)
        out[NY:FACE, :] = jnp.zeros((8, NZ), F32)
        for i, edge in enumerate((low, high)):
            out[NY + i : NY + i + 1, 0:NY] = jnp.where(take, edge[0:1, 0:NY], edge[3:4, 128 - NY :])
    a_ref[FACE : FACE + SUMS, :] = sums_ref[...]


def middle_kernel(
    scale_ref, alpha_ref, leaf_ref, q_ref, near_ref, far_ref, in0_ref, in1_ref, out_ref, local_ref
):
    before = odd("xy") == 1
    near, far = near_ref[...], far_ref[...]
    bz_in = (in0_ref[...], in1_ref[...])
    for a, inner in enumerate((jnp.where(before, near, far), jnp.where(before, far, near))):
        result = dot3(split(inner), bz_in, NT)
        local_ref[a * NP : (a + 1) * NP] = result.reshape(NP, NY, NZ)
    acc = [jnp.zeros((8, 128), F32) for _ in range(TILES)]
    values = vertex_values(scale_ref[LEVELS : LEVELS + 1, :], scale_ref[LEVELS + 1 : LEVELS + 2, :])
    for g, b in enumerate(values):
        for t in range(TILES):
            acc[t] = acc[t] + leaf_ref[g * 8 : g * 8 + 8, t * 128 : (t + 1) * 128] * b
    leaf_alpha = [jnp.sum(acc[t], axis=0, keepdims=True) for t in range(TILES)]
    alpha = []
    side = odd("gz") == 1
    for t in range((LEVELS - 1) * TILES):
        level = t // TILES
        even, odd_at = (sums_row(level, core) + t % TILES for core in range(2))
        row = jnp.where(side, alpha_ref[odd_at : odd_at + 1, :], alpha_ref[even : even + 1, :])
        alpha.append(row * scale_ref[level : level + 1, :])
    for c in range(CHUNKS):
        rows = slice(c * ROWS, (c + 1) * ROWS)
        total = leaf_ref[rows, 0:128] * leaf_alpha[0]
        for t in range(1, TILES):
            total = total + leaf_ref[rows, t * 128 : (t + 1) * 128] * leaf_alpha[t]
        for t in range(len(alpha)):
            total = total + q_ref[rows, t * 128 : (t + 1) * 128] * alpha[t]
        out_ref[rows, :] = total


def final_kernel(scale_ref, alpha_ref, base_ref, local_ref, q_ref, out_ref, sol_ref):
    alpha = alpha_ref[...] * scale_ref[LEVELS - 1 : LEVELS, :]
    start = (LEVELS - 1) * SW
    vm_row = scale_ref[LEVELS : LEVELS + 1, :]
    acc = jnp.zeros((8, ELEMS), F32)
    turned = [jnp.zeros((8, 128), F32) for _ in range(VERTS // 128)]
    for g in range(VERTS // 8):
        rows = slice(g * 8, g * 8 + 8)
        total = base_ref[rows, :]
        for t in range(TILES):
            at = start + t * 128
            total = total + q_ref[rows, at : at + 128] * alpha[t : t + 1, :]
        value = jnp.sum(total, axis=1, keepdims=True)
        lane = iota((8, 128), 0) + (g % 16) * 8
        turned[g // 16] = turned[g // 16] + jnp.where(iota((8, 128), 1) == lane, value, 0.0)
        vertex = (iota((8, ELEMS), 0) + g * 8).astype(F32)
        acc = acc + jnp.where(vertex == vm_row, value, 0.0)
    per_element = jnp.sum(acc, axis=0, keepdims=True)
    mine = (iota((8, ELEMS), 1) >> 4) == iota((8, ELEMS), 0)
    spread = mark((iota((ELEMS, NZ), 0) & (EZ - 1)) == (iota((ELEMS, NZ), 1) >> 3))
    rows = dot_onehot(jnp.where(mine, per_element, 0.0), spread)
    for a in range(EX):
        add = jnp.broadcast_to(rows[a * EY : (a + 1) * EY, None, :], (EY, NP, NZ)).reshape(NY, NZ)
        for i in range(NP):
            out_ref[a * NP + i] = local_ref[a * NP + i] + add
    for k, rows in enumerate(turned):
        sol_ref[:, k * 128 : (k + 1) * 128] = jnp.sum(rows, axis=0, keepdims=True)


LZ = EZ * PTS
LXY = PTS * EY * PTS


def prep_kernel(
    lam_ref, vec_ref, scale_ref, r_ref, za_ref, zb_ref,
    bz0_ref, bz1_ref, in0_ref, in1_ref, f0_ref, f1_ref, k0_ref, k1_ref, inv_ref, s0_ref, s1_ref,
):
    lane = iota((NZ + 8, LZ), 1)
    z = iota((NZ + 8, LZ), 0)
    c, p = div_mod(lane, PTS)
    z = jnp.where(z < NZ, z, jnp.where(z == NZ, -1, jnp.where(z == NZ + 1, NZ, -1000)))
    place = z - NP * c + 1
    _, p10 = div_mod(iota((PTS, LZ), 1), PTS)
    repeat = mark(p10 == iota((PTS, LZ), 0))
    v2 = dot(vec_ref[:, 2, :], repeat)
    bz = jnp.zeros((NZ + 8, LZ), F32)
    for k in range(PTS):
        bz = jnp.where(place == k, v2[k : k + 1, :], bz)
    bz_in = jnp.where((place >= 1) & (place <= NP), bz, 0.0)[0:NZ]
    bz = split(bz)
    bz0_ref[...], bz1_ref[...] = bz
    in0_ref[...], in1_ref[...] = split(bz_in)

    row = iota((8, 128), 0)
    side = odd("gz")
    za, zb = za_ref[0:4, :], inside("gz", zb_ref[...])
    zlow, zhigh = jnp.where(side == 1, za, zb), jnp.where(side == 1, zb, za)
    sides = [
        jnp.where(row == 0, zlow[k : k + 1], jnp.where(row == 1, zhigh[k : k + 1], 0.0)).T
        for k in range(4)
    ]
    own = jnp.concatenate([r_ref[...].reshape(NX * NY, NZ), jnp.concatenate(sides, axis=0)], axis=1)
    s0_ref[...], s1_ref[...] = split(dot3(split(own), bz))

    _, n = div_mod(iota((PTS, LXY), 1), PTS)
    m, _ = div_mod(iota((PTS, LXY), 1), PTS * EY)
    at = iota((PTS, LXY), 0)
    v1 = dot(vec_ref[:, 1, :], mark(n == at))
    v0 = dot(vec_ref[:, 0, :], mark(m == at))
    mb, _ = div_mod(iota((NY, LXY), 1), PTS)
    b = mb & (EY - 1)
    y = iota((NY, LXY), 0)
    place = y - NP * b + 1
    by = jnp.zeros((NY, LXY), F32)
    for j in range(PTS):
        by = jnp.where(place == j, v1[j : j + 1, :], by)
    by_in = jnp.where((place >= 1) & (place <= NP), by, 0.0)
    forward = jnp.concatenate([by * v0[i : i + 1, :] for i in range(PTS)], axis=0)
    f0_ref[...], f1_ref[...] = split(forward.T)
    back = jnp.concatenate([by_in * v0[i : i + 1, :] for i in range(1, NP + 1)], axis=0)
    k0_ref[...], k1_ref[...] = split(back)

    rows40 = EY * PTS
    rb, _ = div_mod(iota((rows40, EY), 0), PTS)
    pick_b = mark(rb == iota((rows40, EY), 1))
    lc, _ = div_mod(iota((EZ, LZ), 1), PTS)
    pick_c = mark(lc == iota((EZ, LZ), 0))
    _, rn = div_mod(iota((rows40, LZ), 0), PTS)
    _, lp = div_mod(iota((rows40, LZ), 1), PTS)
    lam = jnp.zeros((rows40, LZ), F32)
    lam2 = jnp.zeros((rows40, LZ), F32)
    for k in range(PTS):
        lam = jnp.where(rn == k, lam_ref[1:2, k : k + 1], lam)
        lam2 = jnp.where(lp == k, lam_ref[2:3, k : k + 1], lam2)
    for a in range(EX):
        factors = dot(dot(pick_b, scale_ref[a]), pick_c)
        for i in range(PTS):
            inv_ref[a, i * rows40 : (i + 1) * rows40, :] = 1.0 / (
                factors * ((lam_ref[0:1, i : i + 1] + lam) + lam2)
            )


def local_kernel(
    other, s0_ref, s1_ref, face_ref,
    bz0_ref, bz1_ref, f0_ref, f1_ref, k0_ref, k1_ref, inv_ref, out_ref, w0_ref, w1_ref,
):
    face = face_ref[0:FACE, :]
    if other:
        face = inside("xy", face)
    at = odd("xy") if other else 1 - odd("xy")
    points = jnp.concatenate([face[0:NY], face[NY:FACE].T[0:NY]], axis=1)
    edge = split(dot3(split(points), (bz0_ref[...], bz1_ref[...])))
    size = (NP + 1) * NY
    own_from = pl.multiple_of(at * ((NP - 1) * NY), NY)
    own_to = pl.multiple_of((1 - at) * NY, NY)
    edge_to = pl.multiple_of(at * size, NY)
    for s_ref, w_ref, part in ((s0_ref, w0_ref, edge[0]), (s1_ref, w1_ref, edge[1])):
        w_ref[pl.ds(own_to, size), :] = s_ref[pl.ds(own_from, size), :]
        w_ref[pl.ds(edge_to, NY), :] = part
    scaled = dot3((f0_ref[...], f1_ref[...]), (w0_ref[...], w1_ref[...])) * inv_ref[at]
    out_ref[...] = dot3((k0_ref[...], k1_ref[...]), split(scaled))


def shape(*dims):
    return jax.ShapeDtypeStruct(dims, F32)


def cost(flops, size):
    return pl.CostEstimate(flops=flops, bytes_accessed=size, transcendentals=0)


def per_device(
    residual,
    eigen_vectors,
    eigen_values,
    element_scale,
    vertex_map,
    leaf_columns,
    separator_columns,
    separator_mask,
):
    face_a, face_b, partial, aux, points, separators, vectors, values, scale = pl.pallas_call(
        first_kernel,
        out_shape=(
            shape(8 + PARTIALS, 128), shape(4, 128), shape(PARTIALS, 128), shape(8, 128),
            shape(NX, NY, NZ), shape(VERTS, LEVELS * SW),
            shape(PTS, 3, PTS), shape(3, PTS), shape(EX, EY, EZ),
        ),
        in_specs=[pl.BlockSpec(memory_space=pltpu.HBM)] * 7,
        out_specs=(VMEM,) * 9,
        scratch_shapes=[
            pltpu.VMEM((EX, EY, EZ), jnp.int32),
            pltpu.VMEM((1, LEVELS), jnp.int32),
            pltpu.VMEM((VERTS, 128), F32),
            pltpu.SemaphoreType.DMA((CHUNKS + 6,)),
        ],
        compiler_params=pltpu.CompilerParams(vmem_limit_bytes=FIRST_LIMIT),
        cost_estimate=cost(6 * 512 * 512 * 2, 6_500_000),
        name="first",
    )(
        *(
            pltpu.with_memory_space_constraint(x, pltpu.HBM)
            for x in (
                residual, vertex_map, separator_mask, separator_columns,
                eigen_vectors.transpose(1, 0, 2), eigen_values, element_scale,
            )
        )
    )

    def swap(value, axis, bits):
        return lax.ppermute(value, axis, [(i, i ^ bits) for i in range(lax.axis_size(axis))])

    def pairs(value, axis):
        count = lax.axis_size(axis)
        return lax.ppermute(value, axis, [(i, (i + 2 * (i % 2) - 1) % count) for i in range(count)])

    z_a = swap(face_a, "gz", 1)
    z_b = pairs(face_b, "gz")

    total = pl.pallas_call(
        join_kernel,
        out_shape=shape(SUMS, 128),
        in_specs=[VMEM] * 2,
        out_specs=VMEM,
        compiler_params=PARAMS,
        cost_estimate=cost(1000, 50_000),
        name="join",
    )(partial, z_a)

    message_a, message_b = pl.pallas_call(
        edge_kernel,
        out_shape=(shape(FACE + SUMS, NZ), shape(FACE, NZ)),
        in_specs=[VMEM] * 4,
        out_specs=(VMEM, VMEM),
        compiler_params=PARAMS,
        cost_estimate=cost(1000, 100_000),
        name="edges",
    )(points, z_a, z_b, total)

    def widen(value):
        return jnp.pad(value, ((0, SUMS - value.shape[0]), (0, 0)))

    def cross(value, bits):
        count = lax.axis_size("gz") * lax.axis_size("xy")
        partner = lax.axis_size("xy") ^ bits
        return lax.ppermute(value, ("gz", "xy"), [(i, i ^ partner) for i in range(count)])

    two, three = (cross(total[: sums_from(1)], bits) for bits in (3, 2))
    x_a = swap(message_a, "xy", 1)
    total = total + x_a[FACE:] + widen(two + three)
    half = lambda *dims: jax.ShapeDtypeStruct(dims, BF16)
    matrices = pl.pallas_call(
        prep_kernel,
        out_shape=(half(NZ + 8, LZ),) * 2
        + (half(NZ, LZ),) * 2
        + (half(LXY, PTS * NY),) * 2
        + (half(NP * NY, LXY),) * 2
        + (shape(EX, LXY, LZ),)
        + (half(NX * NY, LZ),) * 2,
        in_specs=[VMEM] * 6,
        out_specs=(VMEM,) * 11,
        compiler_params=PARAMS,
        cost_estimate=cost(1_000_000_000, 1_000_000),
        name="prep",
    )(values, vectors, scale, points, z_a, z_b)

    def local(other, face):
        return pl.pallas_call(
            functools.partial(local_kernel, other),
            out_shape=shape(NP * NY, LZ),
            in_specs=[VMEM] * 10,
            out_specs=VMEM,
            scratch_shapes=[pltpu.VMEM((PTS * NY, LZ), BF16)] * 2,
            compiler_params=PARAMS,
            cost_estimate=cost(1_000_000_000, 1_000_000),
            name="local",
        )(*matrices[9:], face, *matrices[:2], *matrices[4:9])

    total, matrices, message_b = lax.optimization_barrier((total, matrices, message_b))
    x_b = pairs(message_b, "xy")
    near = local(False, x_a)
    total = total + widen(cross(total[: sums_from(2)], 6))
    total, near = lax.optimization_barrier((total, near))
    far = local(True, x_b)
    one = cross(total[: sums_from(3)], 8)
    two, three = (cross(total[: sums_from(4)], bits) for bits in (24, 16))
    total = total + widen(one) + widen(two + three)
    total, far = lax.optimization_barrier((total, far))
    last = total[:TILES]
    last = last + (swap(last, "gz", 3) + swap(last, "gz", 7) + swap(last, "gz", 5))

    base, local = pl.pallas_call(
        middle_kernel,
        out_shape=(shape(VERTS, 128), shape(NX, NY, NZ)),
        in_specs=[VMEM] * 8,
        out_specs=(VMEM, VMEM),
        compiler_params=PARAMS,
        cost_estimate=cost(7 * 512 * 512 * 2, 7_000_000),
        name="middle",
    )(aux, total, leaf_columns, separators, near, far, matrices[2], matrices[3])

    out, sol = pl.pallas_call(
        final_kernel,
        out_shape=(shape(NX, NY, NZ), shape(1, VERTS)),
        in_specs=[VMEM] * 5,
        out_specs=(VMEM, VMEM),
        compiler_params=PARAMS,
        cost_estimate=cost(512 * 512 * 2, 1_500_000),
        name="final",
    )(aux, last, base, local, separators)
    return out, sol.reshape(VERTS)


def solution(mesh):
    placed = (
        P("xy", None, "gz"),
        P(),
        P(),
        P("xy", None, "gz"),
        P("xy", None, "gz"),
        P(("gz", "xy"), None),
        P(("gz", "xy"), None),
        P(("gz", "xy"), None),
    )
    return jax.shard_map(
        per_device,
        mesh=mesh,
        in_specs=placed,
        out_specs=(P("xy", None, "gz"), P(("gz", "xy"))),
        check_vma=False,
    )
```

```python
import functools

import jax
import jax.numpy as jnp
from jax import lax
from jax.experimental import pallas as pl
from jax.experimental.pallas import tpu as pltpu
from jax.sharding import PartitionSpec as P

NP = 8
LEVELS = 6
EX, EY, EZ = 2, 4, 16
VERTS = 512
SW = 512
ELEMS = EX * EY * EZ
NX, NY, NZ = EX * NP, EY * NP, EZ * NP
PTS = NP + 2
CHUNKS = 8
ROWS = VERTS // CHUNKS

F32 = jnp.float32
BF16 = jnp.bfloat16
HIGH = lax.Precision.HIGHEST
VMEM = pl.BlockSpec(memory_space=pltpu.VMEM)
FIRST_LIMIT = 40 * 2**20
PARAMS = pltpu.CompilerParams(vmem_limit_bytes=40 * 1024 * 1024)
NN = (((1,), (0,)), ((), ()))
NT = (((1,), (1,)), ((), ()))


def dot(a, b, dims=NN):
    return lax.dot_general(a, b, dims, precision=HIGH, preferred_element_type=F32)


def bdot(a, b, dims=NN):
    return lax.dot_general(a, b, dims, preferred_element_type=F32)


def split(a):
    hi = a.astype(BF16)
    return hi, (a - hi.astype(F32)).astype(BF16)


def dot3(a, b, dims=NN):
    return bdot(a[0], b[0], dims) + (bdot(a[0], b[1], dims) + bdot(a[1], b[0], dims))


def iota(shape, axis):
    return lax.broadcasted_iota(jnp.int32, shape, axis)


def div_mod(values, by):
    quotient = jnp.floor((values.astype(F32) + 0.5) * (1.0 / by)).astype(jnp.int32)
    return quotient, values - quotient * by


def mark(condition):
    return condition.astype(F32)


def split3(a):
    hi = a.astype(BF16).astype(F32)
    rest = a - hi
    mid = rest.astype(BF16).astype(F32)
    return hi, mid, rest - mid


def dot_onehot(a, onehot):
    parts = jnp.concatenate([*split3(a), jnp.zeros_like(a)], axis=0).astype(BF16)
    out = bdot(parts, onehot.astype(BF16))
    return out[0:8] + (out[8:16] + out[16:24])


def odd(axis):
    return lax.rem(lax.axis_index(axis), 2)


def inside(axis, value):
    at = lax.axis_index(axis)
    return jnp.where((at > 0) & (at < lax.axis_size(axis) - 1), value, 0.0)


def factor(level):
    group = 256 if level == LEVELS - 1 else 2 ** (level + 1)
    return float(group) ** (-0.25)


def vertex_values(vm_row, row):
    out = []
    for g in range(VERTS // 8):
        vertex = (iota((8, ELEMS), 0) + g * 8).astype(F32)
        out.append(jnp.sum(jnp.where(vertex == vm_row, row, 0.0), axis=1, keepdims=True))
    return out


TILES = SW // 128
FACE = NY + 8
PARTIALS = LEVELS * TILES
LAST = PARTIALS - TILES
SUMS = 2 * LAST + TILES


def first_kernel(
    r_hbm, vm_hbm, mask_hbm, q_hbm, vec_hbm, lam_hbm, scale_hbm,
    face_a_ref, face_b_ref, aux_ref, r_ref, q_ref, vec_ref, lam_ref, scale_ref,
    v_ref, m_ref, b_ref, sem,
):
    moves = (
        (r_hbm, r_ref), (vm_hbm, v_ref), (mask_hbm, m_ref),
        (vec_hbm, vec_ref), (lam_hbm, lam_ref), (scale_hbm, scale_ref),
    )
    small = [
        pltpu.make_async_copy(src, dst, sem.at[CHUNKS + i]) for i, (src, dst) in enumerate(moves)
    ]
    for copy in small:
        copy.start()
    large = []
    for c in range(CHUNKS):
        rows = pl.ds(c * ROWS, ROWS)
        large.append(pltpu.make_async_copy(q_hbm.at[rows], q_ref.at[rows], sem.at[c]))
        large[-1].start()
    small[1].wait()
    vm = jnp.concatenate([v_ref[0], v_ref[1]], axis=0).astype(F32)
    mine = (iota((8, ELEMS), 1) >> 4) == iota((8, ELEMS), 0)
    spread = mark(iota((EZ, ELEMS), 0) == (iota((EZ, ELEMS), 1) & (EZ - 1)))
    vm_row = jnp.sum(jnp.where(mine, dot_onehot(vm, spread), 0.0), axis=0, keepdims=True)
    small[2].wait()
    scales = []
    for level in range(LEVELS):
        value = m_ref[0:1, level : level + 1].astype(F32) * factor(level)
        scales.append(jnp.broadcast_to(value, (1, 128)))
        aux_ref[level : level + 1, :] = scales[-1]
    aux_ref[LEVELS : LEVELS + 1, :] = vm_row
    small[0].wait()
    sums = []
    for a in range(EX):
        total = r_ref[a * NP]
        for i in range(1, NP):
            total = total + r_ref[a * NP + i]
        sums.append(jnp.sum(total.reshape(EY, NP, NZ), axis=1))
    sums = jnp.concatenate(sums, axis=0) * (1.0 / NP**3)
    gather = mark((iota((NZ, ELEMS), 0) >> 3) == (iota((NZ, ELEMS), 1) & (EZ - 1)))
    means = jnp.sum(jnp.where(mine, dot_onehot(sums, gather), 0.0), axis=0, keepdims=True)
    aux_ref[LEVELS + 1 : LEVELS + 2, :] = means
    for g, value in enumerate(vertex_values(vm_row, means)):
        b_ref[g * 8 : g * 8 + 8, :] = jnp.broadcast_to(value, (8, 128))
    flat = r_ref[...].reshape(NX * NY, NZ)
    row, lane = iota((8, NZ), 0), iota((8, NZ), 1)
    side = odd("gz")
    lane_a = (1 - side) * (NZ - 1)
    lane_b = side * (NZ - 1)
    pick = mark(((row == 0) & (lane == lane_a)) | ((row == 1) & (lane == lane_b)))
    faces = dot(pick, flat, NT)
    for k in range(4):
        face_a_ref[k : k + 1, :] = faces[0:1, k * 128 : (k + 1) * 128]
        face_b_ref[k : k + 1, :] = faces[1:2, k * 128 : (k + 1) * 128]
    acc = [jnp.zeros((8, 128), F32) for _ in range(PARTIALS)]
    for c in range(CHUNKS):
        large[c].wait()
        for g in range(ROWS // 8):
            at = c * ROWS + g * 8
            b = b_ref[at : at + 8, :]
            for t in range(PARTIALS):
                acc[t] = acc[t] + q_ref[at : at + 8, t * 128 : (t + 1) * 128] * b
    for t in range(PARTIALS):
        total = jnp.sum(acc[t], axis=0, keepdims=True) * scales[t // TILES]
        face_a_ref[8 + t : 9 + t, :] = total
    for copy in small[3:]:
        copy.wait()


def sums_row(level, core):
    return TILES + (LEVELS - 2 - level) * 2 * TILES + core * TILES


def sums_from(level):
    return TILES + (LEVELS - 1 - level) * 2 * TILES


def join_kernel(face_a_ref, za_ref, out_ref):
    side = odd("gz") == 1
    mine, other = face_a_ref[8 : 8 + PARTIALS, :], za_ref[8 : 8 + PARTIALS, :]
    out_ref[0:TILES, :] = (mine + other)[LAST:]
    for core, rows in enumerate((jnp.where(side, other, mine), jnp.where(side, mine, other))):
        for level in range(LEVELS - 1):
            at = sums_row(level, core)
            out_ref[at : at + TILES, :] = rows[level * TILES : (level + 1) * TILES]


def edge_kernel(r_ref, za_ref, zb_ref, sums_ref, a_ref, b_ref):
    side = odd("gz")
    za, zb = za_ref[0:4, :], inside("gz", zb_ref[...])
    low = jnp.where(side == 1, za, zb)
    high = jnp.where(side == 1, zb, za)
    turned = odd("xy") == 1
    first, last = r_ref[0], r_ref[NX - 1]
    for out, take in ((a_ref, turned), (b_ref, jnp.logical_not(turned))):
        out[0:NY, :] = jnp.where(take, first, last)
        out[NY:FACE, :] = jnp.zeros((8, NZ), F32)
        for i, edge in enumerate((low, high)):
            out[NY + i : NY + i + 1, 0:NY] = jnp.where(take, edge[0:1, 0:NY], edge[3:4, 128 - NY :])
    a_ref[FACE : FACE + SUMS, :] = sums_ref[...]


def middle_kernel(
    scale_ref, alpha_ref, leaf_ref, q_ref, near_ref, far_ref, in0_ref, in1_ref, out_ref, local_ref
):
    before = odd("xy") == 1
    near, far = near_ref[...], far_ref[...]
    bz_in = (in0_ref[...], in1_ref[...])
    for a, inner in enumerate((jnp.where(before, near, far), jnp.where(before, far, near))):
        result = dot3(split(inner), bz_in, NT)
        local_ref[a * NP : (a + 1) * NP] = result.reshape(NP, NY, NZ)
    acc = [jnp.zeros((8, 128), F32) for _ in range(TILES)]
    values = vertex_values(scale_ref[LEVELS : LEVELS + 1, :], scale_ref[LEVELS + 1 : LEVELS + 2, :])
    for g, b in enumerate(values):
        for t in range(TILES):
            acc[t] = acc[t] + leaf_ref[g * 8 : g * 8 + 8, t * 128 : (t + 1) * 128] * b
    leaf_alpha = [jnp.sum(acc[t], axis=0, keepdims=True) for t in range(TILES)]
    alpha = []
    side = odd("gz") == 1
    for t in range((LEVELS - 1) * TILES):
        level = t // TILES
        even, odd_at = (sums_row(level, core) + t % TILES for core in range(2))
        row = jnp.where(side, alpha_ref[odd_at : odd_at + 1, :], alpha_ref[even : even + 1, :])
        alpha.append(row * scale_ref[level : level + 1, :])
    for c in range(CHUNKS):
        rows = slice(c * ROWS, (c + 1) * ROWS)
        total = leaf_ref[rows, 0:128] * leaf_alpha[0]
        for t in range(1, TILES):
            total = total + leaf_ref[rows, t * 128 : (t + 1) * 128] * leaf_alpha[t]
        for t in range(len(alpha)):
            total = total + q_ref[rows, t * 128 : (t + 1) * 128] * alpha[t]
        out_ref[rows, :] = total


def final_kernel(scale_ref, alpha_ref, base_ref, local_ref, q_ref, out_ref, sol_ref):
    alpha = alpha_ref[...] * scale_ref[LEVELS - 1 : LEVELS, :]
    start = (LEVELS - 1) * SW
    vm_row = scale_ref[LEVELS : LEVELS + 1, :]
    acc = jnp.zeros((8, ELEMS), F32)
    turned = [jnp.zeros((8, 128), F32) for _ in range(VERTS // 128)]
    for g in range(VERTS // 8):
        rows = slice(g * 8, g * 8 + 8)
        total = base_ref[rows, :]
        for t in range(TILES):
            at = start + t * 128
            total = total + q_ref[rows, at : at + 128] * alpha[t : t + 1, :]
        value = jnp.sum(total, axis=1, keepdims=True)
        lane = iota((8, 128), 0) + (g % 16) * 8
        turned[g // 16] = turned[g // 16] + jnp.where(iota((8, 128), 1) == lane, value, 0.0)
        vertex = (iota((8, ELEMS), 0) + g * 8).astype(F32)
        acc = acc + jnp.where(vertex == vm_row, value, 0.0)
    per_element = jnp.sum(acc, axis=0, keepdims=True)
    mine = (iota((8, ELEMS), 1) >> 4) == iota((8, ELEMS), 0)
    spread = mark((iota((ELEMS, NZ), 0) & (EZ - 1)) == (iota((ELEMS, NZ), 1) >> 3))
    rows = dot_onehot(jnp.where(mine, per_element, 0.0), spread)
    for a in range(EX):
        add = jnp.broadcast_to(rows[a * EY : (a + 1) * EY, None, :], (EY, NP, NZ)).reshape(NY, NZ)
        for i in range(NP):
            out_ref[a * NP + i] = local_ref[a * NP + i] + add
    for k, rows in enumerate(turned):
        sol_ref[:, k * 128 : (k + 1) * 128] = jnp.sum(rows, axis=0, keepdims=True)


LZ = EZ * PTS
LXY = PTS * EY * PTS


def prep_kernel(
    lam_ref, vec_ref, scale_ref, r_ref, za_ref, zb_ref,
    bz0_ref, bz1_ref, in0_ref, in1_ref, f0_ref, f1_ref, k0_ref, k1_ref, inv_ref, s0_ref, s1_ref,
):
    lane = iota((NZ + 8, LZ), 1)
    z = iota((NZ + 8, LZ), 0)
    c, p = div_mod(lane, PTS)
    z = jnp.where(z < NZ, z, jnp.where(z == NZ, -1, jnp.where(z == NZ + 1, NZ, -1000)))
    place = z - NP * c + 1
    _, p10 = div_mod(iota((PTS, LZ), 1), PTS)
    repeat = mark(p10 == iota((PTS, LZ), 0))
    v2 = dot(vec_ref[:, 2, :], repeat)
    bz = jnp.zeros((NZ + 8, LZ), F32)
    for k in range(PTS):
        bz = jnp.where(place == k, v2[k : k + 1, :], bz)
    bz_in = jnp.where((place >= 1) & (place <= NP), bz, 0.0)[0:NZ]
    bz = split(bz)
    bz0_ref[...], bz1_ref[...] = bz
    in0_ref[...], in1_ref[...] = split(bz_in)

    row = iota((8, 128), 0)
    side = odd("gz")
    za, zb = za_ref[0:4, :], inside("gz", zb_ref[...])
    zlow, zhigh = jnp.where(side == 1, za, zb), jnp.where(side == 1, zb, za)
    sides = [
        jnp.where(row == 0, zlow[k : k + 1], jnp.where(row == 1, zhigh[k : k + 1], 0.0)).T
        for k in range(4)
    ]
    own = jnp.concatenate([r_ref[...].reshape(NX * NY, NZ), jnp.concatenate(sides, axis=0)], axis=1)
    s0_ref[...], s1_ref[...] = split(dot3(split(own), bz))

    _, n = div_mod(iota((PTS, LXY), 1), PTS)
    m, _ = div_mod(iota((PTS, LXY), 1), PTS * EY)
    at = iota((PTS, LXY), 0)
    v1 = dot(vec_ref[:, 1, :], mark(n == at))
    v0 = dot(vec_ref[:, 0, :], mark(m == at))
    mb, _ = div_mod(iota((NY, LXY), 1), PTS)
    b = mb & (EY - 1)
    y = iota((NY, LXY), 0)
    place = y - NP * b + 1
    by = jnp.zeros((NY, LXY), F32)
    for j in range(PTS):
        by = jnp.where(place == j, v1[j : j + 1, :], by)
    by_in = jnp.where((place >= 1) & (place <= NP), by, 0.0)
    forward = jnp.concatenate([by * v0[i : i + 1, :] for i in range(PTS)], axis=0)
    f0_ref[...], f1_ref[...] = split(forward.T)
    back = jnp.concatenate([by_in * v0[i : i + 1, :] for i in range(1, NP + 1)], axis=0)
    k0_ref[...], k1_ref[...] = split(back)

    rows40 = EY * PTS
    rb, _ = div_mod(iota((rows40, EY), 0), PTS)
    pick_b = mark(rb == iota((rows40, EY), 1))
    lc, _ = div_mod(iota((EZ, LZ), 1), PTS)
    pick_c = mark(lc == iota((EZ, LZ), 0))
    _, rn = div_mod(iota((rows40, LZ), 0), PTS)
    _, lp = div_mod(iota((rows40, LZ), 1), PTS)
    lam = jnp.zeros((rows40, LZ), F32)
    lam2 = jnp.zeros((rows40, LZ), F32)
    for k in range(PTS):
        lam = jnp.where(rn == k, lam_ref[1:2, k : k + 1], lam)
        lam2 = jnp.where(lp == k, lam_ref[2:3, k : k + 1], lam2)
    for a in range(EX):
        factors = dot(dot(pick_b, scale_ref[a]), pick_c)
        for i in range(PTS):
            inv_ref[a, i * rows40 : (i + 1) * rows40, :] = 1.0 / (
                factors * ((lam_ref[0:1, i : i + 1] + lam) + lam2)
            )


def local_kernel(
    other, s0_ref, s1_ref, face_ref,
    bz0_ref, bz1_ref, f0_ref, f1_ref, k0_ref, k1_ref, inv_ref, out_ref, w0_ref, w1_ref,
):
    face = face_ref[0:FACE, :]
    if other:
        face = inside("xy", face)
    at = odd("xy") if other else 1 - odd("xy")
    points = jnp.concatenate([face[0:NY], face[NY:FACE].T[0:NY]], axis=1)
    edge = split(dot3(split(points), (bz0_ref[...], bz1_ref[...])))
    size = (NP + 1) * NY
    own_from = pl.multiple_of(at * ((NP - 1) * NY), NY)
    own_to = pl.multiple_of((1 - at) * NY, NY)
    edge_to = pl.multiple_of(at * size, NY)
    for s_ref, w_ref, part in ((s0_ref, w0_ref, edge[0]), (s1_ref, w1_ref, edge[1])):
        w_ref[pl.ds(own_to, size), :] = s_ref[pl.ds(own_from, size), :]
        w_ref[pl.ds(edge_to, NY), :] = part
    scaled = dot3((f0_ref[...], f1_ref[...]), (w0_ref[...], w1_ref[...])) * inv_ref[at]
    out_ref[...] = dot3((k0_ref[...], k1_ref[...]), split(scaled))


def shape(*dims):
    return jax.ShapeDtypeStruct(dims, F32)


def cost(flops, size):
    return pl.CostEstimate(flops=flops, bytes_accessed=size, transcendentals=0)


def per_device(
    residual,
    eigen_vectors,
    eigen_values,
    element_scale,
    vertex_map,
    leaf_columns,
    separator_columns,
    separator_mask,
):
    face_a, face_b, aux, points, separators, vectors, values, scale = pl.pallas_call(
        first_kernel,
        out_shape=(
            shape(8 + PARTIALS, 128), shape(4, 128), shape(8, 128),
            shape(NX, NY, NZ), shape(VERTS, LEVELS * SW),
            shape(PTS, 3, PTS), shape(3, PTS), shape(EX, EY, EZ),
        ),
        in_specs=[pl.BlockSpec(memory_space=pltpu.HBM)] * 7,
        out_specs=(VMEM,) * 8,
        scratch_shapes=[
            pltpu.VMEM((EX, EY, EZ), jnp.int32),
            pltpu.VMEM((1, LEVELS), jnp.int32),
            pltpu.VMEM((VERTS, 128), F32),
            pltpu.SemaphoreType.DMA((CHUNKS + 6,)),
        ],
        compiler_params=pltpu.CompilerParams(vmem_limit_bytes=FIRST_LIMIT),
        cost_estimate=cost(6 * 512 * 512 * 2, 6_500_000),
        name="first",
    )(
        *(
            pltpu.with_memory_space_constraint(x, pltpu.HBM)
            for x in (
                residual, vertex_map, separator_mask, separator_columns,
                eigen_vectors.transpose(1, 0, 2), eigen_values, element_scale,
            )
        )
    )

    def swap(value, axis, bits):
        return lax.ppermute(value, axis, [(i, i ^ bits) for i in range(lax.axis_size(axis))])

    def pairs(value, axis):
        count = lax.axis_size(axis)
        return lax.ppermute(value, axis, [(i, (i + 2 * (i % 2) - 1) % count) for i in range(count)])

    z_a = swap(face_a, "gz", 1)
    z_b = pairs(face_b, "gz")

    total = pl.pallas_call(
        join_kernel,
        out_shape=shape(SUMS, 128),
        in_specs=[VMEM] * 2,
        out_specs=VMEM,
        compiler_params=PARAMS,
        cost_estimate=cost(1000, 50_000),
        name="join",
    )(face_a, z_a)

    message_a, message_b = pl.pallas_call(
        edge_kernel,
        out_shape=(shape(FACE + SUMS, NZ), shape(FACE, NZ)),
        in_specs=[VMEM] * 4,
        out_specs=(VMEM, VMEM),
        compiler_params=PARAMS,
        cost_estimate=cost(1000, 100_000),
        name="edges",
    )(points, z_a, z_b, total)

    def widen(value):
        return jnp.pad(value, ((0, SUMS - value.shape[0]), (0, 0)))

    def cross(value, bits):
        count = lax.axis_size("gz") * lax.axis_size("xy")
        partner = lax.axis_size("xy") ^ bits
        return lax.ppermute(value, ("gz", "xy"), [(i, i ^ partner) for i in range(count)])

    two, three = (cross(total[: sums_from(1)], bits) for bits in (3, 2))
    x_a = swap(message_a, "xy", 1)
    total = total + x_a[FACE:] + widen(two + three)
    half = lambda *dims: jax.ShapeDtypeStruct(dims, BF16)
    matrices = pl.pallas_call(
        prep_kernel,
        out_shape=(half(NZ + 8, LZ),) * 2
        + (half(NZ, LZ),) * 2
        + (half(LXY, PTS * NY),) * 2
        + (half(NP * NY, LXY),) * 2
        + (shape(EX, LXY, LZ),)
        + (half(NX * NY, LZ),) * 2,
        in_specs=[VMEM] * 6,
        out_specs=(VMEM,) * 11,
        compiler_params=PARAMS,
        cost_estimate=cost(1_000_000_000, 1_000_000),
        name="prep",
    )(values, vectors, scale, points, z_a, z_b)

    def local(other, face):
        return pl.pallas_call(
            functools.partial(local_kernel, other),
            out_shape=shape(NP * NY, LZ),
            in_specs=[VMEM] * 10,
            out_specs=VMEM,
            scratch_shapes=[pltpu.VMEM((PTS * NY, LZ), BF16)] * 2,
            compiler_params=PARAMS,
            cost_estimate=cost(1_000_000_000, 1_000_000),
            name="local",
        )(*matrices[9:], face, *matrices[:2], *matrices[4:9])

    total, matrices, message_b = lax.optimization_barrier((total, matrices, message_b))
    x_b = pairs(message_b, "xy")
    near = local(False, x_a)
    total = total + widen(cross(total[: sums_from(2)], 6))
    total, near = lax.optimization_barrier((total, near))
    far = local(True, x_b)
    one = cross(total[: sums_from(3)], 8)
    two, three = (cross(total[: sums_from(4)], bits) for bits in (24, 16))
    total = total + widen(one) + widen(two + three)
    total, far = lax.optimization_barrier((total, far))
    last = total[:TILES]
    last = last + (swap(last, "gz", 3) + swap(last, "gz", 7) + swap(last, "gz", 5))

    base, local = pl.pallas_call(
        middle_kernel,
        out_shape=(shape(VERTS, 128), shape(NX, NY, NZ)),
        in_specs=[VMEM] * 8,
        out_specs=(VMEM, VMEM),
        compiler_params=PARAMS,
        cost_estimate=cost(7 * 512 * 512 * 2, 7_000_000),
        name="middle",
    )(aux, total, leaf_columns, separators, near, far, matrices[2], matrices[3])

    out, sol = pl.pallas_call(
        final_kernel,
        out_shape=(shape(NX, NY, NZ), shape(1, VERTS)),
        in_specs=[VMEM] * 5,
        out_specs=(VMEM, VMEM),
        compiler_params=PARAMS,
        cost_estimate=cost(512 * 512 * 2, 1_500_000),
        name="final",
    )(aux, last, base, local, separators)
    return out, sol.reshape(VERTS)


def solution(mesh):
    placed = (
        P("xy", None, "gz"),
        P(),
        P(),
        P("xy", None, "gz"),
        P("xy", None, "gz"),
        P(("gz", "xy"), None),
        P(("gz", "xy"), None),
        P(("gz", "xy"), None),
    )
    return jax.shard_map(
        per_device,
        mesh=mesh,
        in_specs=placed,
        out_specs=(P("xy", None, "gz"), P(("gz", "xy"))),
        check_vma=False,
    )
```
